256 devices in a mesh: grp: 2 (over core), ctx: 64 (over x, z_lo, y), hd: 2 (over z_hi).
Axes of the slice: x: 4, y: 4, z: 8 (z_hi: 2, z_lo: 4; z = z_hi * 4 + z_lo), core: 2. Of those that a mesh axis runs over, the one named last changes fastest.
Arguments:
- video_q: bfloat16 [8192, 24, 128], P(('ctx', 'hd'), 'grp'), may hold values from -6 to 6
- video_k: bfloat16 [8192, 24, 128], P(('ctx', 'hd'), 'grp'), may hold values from -6 to 6
- video_v: bfloat16 [8192, 24, 128], P(('ctx', 'hd'), 'grp'), may hold values from -6 to 6
- positions: int32 [3, 8192], P(None, ('ctx', 'hd')), may hold values from 0 to 31, as said below
- text_q: bfloat16 [256, 24, 128], P(None, ('grp', 'hd')), may hold values from -16 to 16
- text_k: bfloat16 [256, 24, 128], P(None, ('grp', 'hd')), may hold values from -16 to 16
- text_v: bfloat16 [256, 24, 128], P(None, ('grp', 'hd')), may hold values from -6 to 6
- text_count: int32 [1], replicated, may hold values from 64 to 256
Outputs:
- video_out: bfloat16 [8192, 24, 128], P(('ctx', 'hd'), 'grp')
- text_out: bfloat16 [256, 24, 128], P('ctx', ('grp', 'hd'))
The draws below stay inside these ranges and needn't reach their ends.
Inputs may be any that keep to these rules, and one draw needn't show every extreme that they name: `positions`: column n holds the frame, row and column of video token n; the columns are distinct cells of a grid of 32 frames of 16 by 16 cells.
All inputs are finite; a program needn't handle non-finite values.
Results may differ from the reference program's by a relative error of at most 0.0073.
Values may be sent and summed in bfloat16 or wider, within the bound.
No kernel may reach another device: no remote copies, remote signals or barrier semaphores. Data moves between devices by JAX's collectives and lax.ppermute only.
A program may use at most 128 MiB of HBM per device.

```python
import math
import jax
import jax.numpy as jnp
from jax import lax

HEADS = 24
HD = 128
TXT = 256
GRID_H = 16
GRID_W = 16
TOKENS = 8192


def text_pair(key):
    array_shape = (TXT, HEADS, HD)
    keys_base = jnp.clip(jax.random.normal(jax.random.fold_in(key, 101), array_shape, jnp.float32), -3.2, 3.2)
    query_base = jnp.clip(jax.random.normal(jax.random.fold_in(key, 102), array_shape, jnp.float32), -3.2, 3.2)
    return (query_base, keys_base)


def draw_text_q(key, part):
    return text_pair(key)[0].astype(jnp.bfloat16)


def draw_text_k(key, part):
    return text_pair(key)[1].astype(jnp.bfloat16)


def draw_positions(key, part):
    ordering = jax.random.permutation(jax.random.fold_in(key, 7), TOKENS)
    cell_count = GRID_H * GRID_W
    frame_at = ordering // cell_count
    row_at = ordering // GRID_W % GRID_H
    column = ordering % GRID_W
    return jnp.stack([frame_at, row_at, column]).astype(jnp.int32)


def steps_of(stream_key, extent, shards, least, high):
    level = 1.0
    for axis_at, shards_of in shards:
        heights = jax.random.uniform(jax.random.fold_in(jax.random.fold_in(stream_key, 6), axis_at), (shards_of,), jnp.float32, least / len(shards), high / len(shards))
        level = level * jnp.repeat(jnp.exp(heights), extent[axis_at] // shards_of).reshape((-1,) + (1,) * (len(extent) - 1 - axis_at))
    return level


def gaussian(own_key, extent, deviation, bound, cuts=(), held_as=jnp.bfloat16):
    loudness = steps_of(own_key, extent, cuts, -0.22, 0.18) if cuts else 1.0
    entries = jax.random.normal(own_key, extent, jnp.float32) * deviation * loudness
    return jnp.minimum(jnp.maximum(entries, -bound), bound).astype(held_as)


def setup_inputs(seed: int = 0) -> dict:
    arg_keys = jax.random.split(jax.random.key(seed), 9)
    return {
        "video_q": gaussian(arg_keys[0], (TOKENS, HEADS, HD), 1.0, 6.0, ((0, 128), (1, 2))),
        "video_k": gaussian(arg_keys[1], (TOKENS, HEADS, HD), 1.0, 6.0, ((0, 128), (1, 2))),
        "video_v": gaussian(arg_keys[2], (TOKENS, HEADS, HD), 1.0, 6.0, ((0, 128), (1, 2))),
        "positions": draw_positions(jax.random.fold_in(arg_keys[8], 71), 0),
        "text_q": draw_text_q(jax.random.fold_in(arg_keys[8], 71), 0),
        "text_k": draw_text_k(jax.random.fold_in(arg_keys[8], 71), 0),
        "text_v": gaussian(arg_keys[6], (TXT, HEADS, HD), 1.0, 6.0, ((1, 4),)),
        "text_count": jax.random.randint(arg_keys[7], (1,), TXT // 4, TXT + 1).astype(jnp.int32),
    }


THETA = 256.0

def rotate(tokens_in, positions):
    head_dim = tokens_in.shape[-1]
    band_t = head_dim // 8
    band_h = (head_dim - band_t) // 2
    band_w = head_dim - band_t - band_h
    values = tokens_in.astype(jnp.float32)
    pieces = []
    offset = 0
    for axis_index, band_size in ((0, band_t), (1, band_h), (2, band_w)):
        half_size = band_size // 2
        frequency = THETA ** (-2.0 * jnp.arange(half_size, dtype=jnp.float32) / band_size)
        angles = positions[axis_index].astype(jnp.float32)[:, None] * frequency[None, :]
        cos_table = jnp.cos(angles)[:, None, :]
        sin_table = jnp.sin(angles)[:, None, :]
        lower_half = values[:, :, offset:offset + half_size]
        upper_half = values[:, :, offset + half_size:offset + band_size]
        pieces.append(lower_half * cos_table - upper_half * sin_table)
        pieces.append(upper_half * cos_table + lower_half * sin_table)
        offset += band_size
    return jnp.concatenate(pieces, axis=-1).astype(jnp.bfloat16)

def reference(video_q, video_k, video_v, positions, text_q, text_k, text_v, text_count):
    rot_q = rotate(video_q, positions)
    rot_k = rotate(video_k, positions)
    queries = jnp.moveaxis(jnp.concatenate([rot_q, text_q], axis=0), 1, 0)
    keys_all = jnp.moveaxis(jnp.concatenate([rot_k, text_k], axis=0), 1, 0)
    values_all = jnp.moveaxis(jnp.concatenate([video_v, text_v], axis=0), 1, 0)
    live = jnp.concatenate([jnp.ones((TOKENS,), dtype=bool), jnp.arange(TXT, dtype=jnp.int32) < text_count[0]])
    scale = 1.0 / math.sqrt(HD)

    def head_attention(operands):
        q_head, k_head, v_head = operands
        scores = jnp.dot(q_head, k_head.T, preferred_element_type=jnp.float32) * scale
        scores = jnp.where(live[None, :], scores, -jnp.inf)
        peak = lax.optimization_barrier(jnp.max(scores, axis=1, keepdims=True))
        probs = jnp.exp(scores - peak)
        total = lax.optimization_barrier(jnp.sum(probs, axis=1, keepdims=True))
        mixed = jnp.dot(probs.astype(jnp.bfloat16), v_head, preferred_element_type=jnp.float32)
        return (mixed / total).astype(jnp.bfloat16)
    attended = jnp.moveaxis(lax.map(head_attention, (queries, keys_all, values_all)), 0, 1)
    video_out = attended[:TOKENS]
    text_out = attended[TOKENS:]
    return (video_out, text_out)
```

```python
import functools
import math

import jax
import jax.numpy as jnp
import numpy as np
from jax import lax
from jax.experimental import pallas as pl
from jax.experimental.pallas import tpu as pltpu
from jax.sharding import Mesh
from jax.sharding import PartitionSpec as P

THETA = 256.0
HD = 128
SCALE2 = math.log2(math.e) / math.sqrt(HD)

EVEN = (0, 2, -2, 4)
ODD = (1, -1, 3, -3)
ZAXES = ("grp", "za", "zp", "zb")


def z_index(c, z):
    return ((c * 2 + (z // 2) % 2) * 2 + z % 2) * 2 + z // 4


def moves(z, c):
    return EVEN if z % 2 == c else ODD


def z_perm(m, back):
    pairs = []
    for c in range(2):
        for z in range(8):
            there = z_index(z % 2, (z + moves(z, c)[m]) % 8)
            here = z_index(c, z)
            pairs.append((there, here) if back else (here, there))
    return pairs


GROUP_OF = np.array([[[((z + d) % 8) // 2 for d in moves(z, c)] for c in range(2)] for z in range(8)], np.int32)
MESSAGE_OF = np.argsort(GROUP_OF, axis=-1).astype(np.int32)


def rotary_constants():
    freq = np.zeros((3, HD), np.float32)
    swap = np.zeros((HD, HD), np.float32)
    band_t = HD // 8
    band_h = (HD - band_t) // 2
    offset = 0
    for axis, band in enumerate((band_t, band_h, HD - band_t - band_h)):
        half = band // 2
        f = THETA ** (-2.0 * np.arange(half) / band)
        freq[axis, offset : offset + half] = f
        freq[axis, offset + half : offset + band] = f
        for i in range(half):
            swap[offset + half + i, offset + i] = -1.0
            swap[offset + i, offset + half + i] = 1.0
        offset += band
    return freq, swap


FREQ, SWAP = rotary_constants()


def shift(v, axis, step):
    return lax.ppermute(v, axis, [(i, (i + step) % 4) for i in range(4)])


def other_core(v):
    return lax.ppermute(v, "grp", [(0, 1), (1, 0)])


def z_send(v, m):
    return lax.ppermute(v, ZAXES, z_perm(m, False))


def z_return(v, m):
    return lax.ppermute(v, ZAXES, z_perm(m, True))


QROWS = 272
OWN_TEXT = 256


def attend_body(n_parts, has_text, has_carry, keys_step, *refs):
    refs = list(refs)
    count_ref = refs.pop(0) if has_text else None
    q_own, q_other = refs[:2]
    parts = refs[2 : 2 + n_parts]
    refs = refs[2 + n_parts :]
    text = refs.pop(0) if has_text else None
    carry = refs.pop(0) if has_carry else None
    out = refs.pop(0)
    nt = (((1,), (1,)), ((), ()))
    blocks = []
    for part in parts:
        pieces = part.shape[0]
        for i in range(0, pieces, keys_step):
            blocks.append((part, i, min(keys_step, pieces - i)))
    for tile, q_ref in enumerate((q_own, q_other)):
        q = q_ref[0]
        if has_carry:
            acc, top, total = carry[tile, 0, 0], carry[tile, 1, 0][:, :1], carry[tile, 1, 0][:, 64:65]
        else:
            acc = top = total = None

        def update(s, v, acc, top, total):
            peak = jnp.max(s, axis=1, keepdims=True)
            if top is None:
                new = peak
            else:
                new = jnp.maximum(top, peak)
            p = jnp.exp2(s - new)
            add = jnp.sum(p, axis=1, keepdims=True)
            mixed = jnp.dot(p.astype(jnp.bfloat16), v, preferred_element_type=jnp.float32)
            if top is None:
                return mixed, new, add
            alpha = jnp.exp2(top - new)
            return acc * alpha + mixed, new, total * alpha + add

        for part, i, n in blocks:
            k = part[i : i + n, 0, 0].reshape(n * part.shape[3], HD)
            v = part[i : i + n, 1, 0].reshape(n * part.shape[3], HD)
            s = lax.dot_general(q, k, nt, preferred_element_type=jnp.float32) * SCALE2
            acc, top, total = update(s, v, acc, top, total)
        if has_text:
            k, v = text[0, :128], text[0, 128:256]
            s = lax.dot_general(q, k, nt, preferred_element_type=jnp.float32) * SCALE2
            live = lax.broadcasted_iota(jnp.int32, s.shape, 1) < count_ref[0]
            s = jnp.where(live, s, -jnp.inf)
            acc, top, total = update(s, v, acc, top, total)
        out[tile, 0, 0] = acc
        lane = lax.broadcasted_iota(jnp.int32, acc.shape, 1)
        out[tile, 1, 0] = jnp.where(lane < 64, top, total)


def attend(q_own, q_other, parts, text=None, count=None, carry=None, keys_step=4):
    has_text, has_carry = text is not None, carry is not None
    q_spec = pl.BlockSpec((1, QROWS, HD), lambda h, *_: (h, 0, 0))
    state_spec = pl.BlockSpec((2, 2, 1, QROWS, HD), lambda h, *_: (0, 0, h, 0, 0))
    in_specs, args = [q_spec, q_spec], [q_own, q_other]
    keys = 0
    for part in parts:
        in_specs.append(pl.BlockSpec((part.shape[0], 2, 1) + part.shape[3:], lambda h, *_: (0, 0, h, 0, 0)))
        args.append(part)
        keys += part.shape[0] * part.shape[3]
    if has_text:
        in_specs.append(pl.BlockSpec((1, text.shape[1], HD), lambda h, *_: (h, 0, 0)))
        args.append(text)
        keys += 128
    if has_carry:
        in_specs.append(state_spec)
        args.append(carry)
    flops = 4 * 3 * 2 * QROWS * keys * HD
    return pl.pallas_call(
        functools.partial(attend_body, len(parts), has_text, has_carry, keys_step),
        out_shape=jax.ShapeDtypeStruct((2, 2, 3, QROWS, HD), jnp.float32),
        grid_spec=pltpu.PrefetchScalarGridSpec(
            num_scalar_prefetch=1 if has_text else 0,
            grid=(3,),
            in_specs=in_specs,
            out_specs=state_spec,
        ),
        compiler_params=pltpu.CompilerParams(vmem_limit_bytes=40 * 1024 * 1024),
        cost_estimate=pl.CostEstimate(
            flops=flops, bytes_accessed=keys * 3 * 512 + 3400000, transcendentals=3 * 2 * QROWS * keys
        ),
        name="attend",
    )(*(([count] if has_text else []) + args))


def merge_body(mine, theirs, out):
    top1, top2 = mine[0, 1, 0][:, :1], theirs[1, 0][:, :1]
    total1, total2 = mine[0, 1, 0][:, 64:65], theirs[1, 0][:, 64:65]
    top = jnp.maximum(top1, top2)
    w1, w2 = jnp.exp2(top1 - top), jnp.exp2(top2 - top)
    inv = 1.0 / (total1 * w1 + total2 * w2)
    o = (mine[0, 0, 0] * (w1 * inv) + theirs[0, 0] * (w2 * inv)).astype(jnp.bfloat16)
    for m in range(4):
        out[m, 0, :64] = o[m * 64 : (m + 1) * 64]
        out[m, 0, 64:80] = o[OWN_TEXT : OWN_TEXT + 16]


def merge(mine, theirs):
    return pl.pallas_call(
        merge_body,
        out_shape=jax.ShapeDtypeStruct((4, 3, 80, HD), jnp.bfloat16),
        grid=(3,),
        in_specs=[
            pl.BlockSpec((1, 2, 1, QROWS, HD), lambda h: (0, 0, h, 0, 0)),
            pl.BlockSpec((2, 1, QROWS, HD), lambda h: (0, h, 0, 0)),
        ],
        out_specs=pl.BlockSpec((4, 1, 80, HD), lambda h: (0, h, 0, 0)),
        name="merge",
    )(mine, theirs)


def spread(block, first, second):
    right = shift(block, first, 1)
    left = shift(block, first, -1)
    far = jnp.stack([shift(right[0], first, 1), shift(left[1], first, -1)])
    line = jnp.stack([block, right, left, far])
    right2 = shift(line, second, 1)
    left2 = shift(line, second, -1)
    far_a = shift(right2[:2], second, 1)
    far_b = shift(left2[2:], second, -1)
    return line, right2, left2, far_a, far_b


def local(video_q, video_k, video_v, positions, text_q, text_k, text_v, text_count):
    core = lax.axis_index("grp")
    zb, za, zp = lax.axis_index("zb"), lax.axis_index("za"), lax.axis_index("zp")
    z = zb * 4 + za * 2 + zp
    group_of = jnp.asarray(GROUP_OF)[z, core]
    message_of = jnp.asarray(MESSAGE_OF)[z, core]

    angles = jnp.sum(positions.astype(jnp.float32)[:, :, None] * FREQ[:, None, :], axis=0)
    cos, sin = jnp.cos(angles), jnp.sin(angles)

    def rotate(x):
        x = jnp.transpose(x, (1, 0, 2))
        swapped = jnp.einsum("htd,de->hte", x, jnp.asarray(SWAP, jnp.bfloat16), preferred_element_type=jnp.float32)
        return (x.astype(jnp.float32) * cos + swapped * sin).astype(jnp.bfloat16)

    k = rotate(video_k).reshape(4, 3, 64, HD)
    v = jnp.transpose(video_v, (1, 0, 2)).reshape(4, 3, 64, HD)
    q = rotate(video_q).reshape(4, 3, 64, HD)
    kv = jnp.stack([k, v], axis=1)
    pick = lambda a, m: lax.dynamic_index_in_dim(a, group_of[m], 0, keepdims=False)
    kv_in = [z_send(pick(kv, m), m) for m in range(4)]
    q_in = [z_send(pick(q, m), m) for m in range(4)]

    half = zp
    heads = lambda a: lax.dynamic_slice_in_dim(a, za * 3, 3, 1)
    x, y = lax.axis_index("x"), lax.axis_index("y")

    def text_for(c):
        tk = lax.dynamic_slice_in_dim(heads(text_k), c * 128, 128, 0)
        tv = lax.dynamic_slice_in_dim(heads(text_v), c * 128, 128, 0)
        rows = [
            lax.dynamic_slice_in_dim(heads(text_q), (x * 16 + (c + 2 * t) * 4 + y) * 4, 4, 0) for t in range(2)
        ]
        block = jnp.concatenate([tk, tv] + rows + [jnp.zeros((8, 3, HD), jnp.bfloat16)], axis=0)
        return jnp.transpose(block, (1, 0, 2))

    text = jnp.where(core == half, text_for(core), other_core(text_for(1 - core)))
    count = jnp.clip(text_count - core * 128, 0, 128)

    q_own = jnp.concatenate(q_in + [text[:, 256:272]], axis=1)
    q_other = other_core(q_own)

    first = jnp.concatenate(kv_in[:2], axis=2)
    second = jnp.concatenate(kv_in[2:], axis=2)
    line_a, right_a, left_a, far_a0, far_a1 = spread(first, "x", "y")
    line_b, right_b, left_b, far_b0, far_b1 = spread(second, "y", "x")
    state = attend(q_own, q_other, [line_a, line_b], text=text, count=count)
    state = attend(q_own, q_other, [right_a, left_a, right_b, left_b], carry=state)
    state = attend(q_own, q_other, [far_a0, far_a1, far_b0, far_b1], carry=state)

    theirs = other_core(state[1])
    done = merge(state, theirs)
    back = jnp.stack([z_return(done[m], m) for m in range(4)])
    ordered = jnp.stack([lax.dynamic_index_in_dim(back, message_of[j], 0, keepdims=False) for j in range(4)])
    video_out = jnp.transpose(ordered[:, :, :64].reshape(12, 64, HD), (1, 0, 2))
    texts = lax.dynamic_slice(ordered, (zb * 2, 0, 64 + za * 4, 0), (2, 3, 4, HD))
    text_out = jnp.transpose(texts.reshape(6, 4, HD), (1, 0, 2))
    return video_out, text_out


def solution(mesh):
    fine = Mesh(mesh.devices.reshape(2, 4, 2, 2, 4, 2), ("grp", "x", "za", "zp", "y", "zb"))
    ctx = ("x", "za", "zp", "y")
    tokens = P(ctx + ("zb",), "grp", None)
    text = P(None, ("grp", "zb"), None)
    return jax.shard_map(
        local,
        mesh=fine,
        in_specs=(tokens, tokens, tokens, P(None, ctx + ("zb",)), text, text, text, P()),
        out_specs=(tokens, P(ctx, ("grp", "zb"), None)),
        check_vma=False,
    )
```

```python
import functools
import math

import jax
import jax.numpy as jnp
import numpy as np
from jax import lax
from jax.experimental import pallas as pl
from jax.experimental.pallas import tpu as pltpu
from jax.sharding import Mesh
from jax.sharding import PartitionSpec as P

THETA = 256.0
HD = 128
SCALE2 = math.log2(math.e) / math.sqrt(HD)
NT = (((1,), (1,)), ((), ()))
TN = (((0,), (0,)), ((), ()))

EVEN = (0, 2, -2, 4)
ODD = (1, -1, 3, -3)
ZAXES = ("grp", "za", "zp", "zb")
OWN, TEXT, OTHER = 256, 16, 256
HALF = OWN + TEXT
QROWS = OWN + TEXT + OTHER
PACK = 128 + 128 + TEXT


def z_index(c, z):
    return ((c * 2 + (z // 2) % 2) * 2 + z % 2) * 2 + z // 4


def z_perm(m, back):
    pairs = []
    for c in range(2):
        for z in range(8):
            d = EVEN[m] if z % 2 == c else ODD[m]
            there = z_index(z % 2, (z + d) % 8)
            here = z_index(c, z)
            pairs.append((there, here) if back else (here, there))
    return pairs


def rotary_constants():
    freq = np.zeros((3, HD), np.float32)
    swap = np.zeros((HD, HD), np.float32)
    band_t = HD // 8
    band_h = (HD - band_t) // 2
    offset = 0
    for axis, band in enumerate((band_t, band_h, HD - band_t - band_h)):
        half = band // 2
        f = THETA ** (-2.0 * np.arange(half) / band)
        freq[axis, offset : offset + half] = f
        freq[axis, offset + half : offset + band] = f
        for i in range(half):
            swap[offset + half + i, offset + i] = -1.0
            swap[offset + i, offset + half + i] = 1.0
        offset += band
    return freq, swap


FREQ, SWAP = rotary_constants()


def shift(v, axis, step):
    return lax.ppermute(v, axis, [(i, (i + step) % 4) for i in range(4)])


def other_core(v):
    return lax.ppermute(v, "grp", [(0, 1), (1, 0)])


def z_send(v, m):
    return lax.ppermute(v, ZAXES, z_perm(m, False))


def z_return(v, m):
    return lax.ppermute(v, ZAXES, z_perm(m, True))


def place():
    core = lax.axis_index("grp")
    za, zp, zb = lax.axis_index("za"), lax.axis_index("zp"), lax.axis_index("zb")
    return core, zb * 4 + za * 2 + zp, za, zp, zb


def group_of(m, core, z, zp):
    d = jnp.where(zp == core, EVEN[m] + 8, ODD[m] + 8)
    return lax.rem(z + d, 8) // 2


def prepare_body(q_ref, k_ref, v_ref, pos_ref, tq_ref, tk_ref, tv_ref, freq_ref, swap_ref, *outs):
    core, z, za, zp, zb = place()
    y = lax.axis_index("y")
    x = lax.axis_index("x")
    messages, own_text, send_text = outs[:4], outs[4], outs[5]
    angles = lax.dot_general(
        pos_ref[...].astype(jnp.float32),
        freq_ref[...],
        TN,
        precision=lax.Precision.HIGHEST,
        preferred_element_type=jnp.float32,
    )
    cos, sin = jnp.cos(angles), jnp.sin(angles)
    swap = swap_ref[...]

    def rotate(block):
        swapped = jnp.dot(block.reshape(3 * 64, HD), swap, preferred_element_type=jnp.float32)
        return (block.astype(jnp.float32) * cos + swapped.reshape(3, 64, HD) * sin).astype(jnp.bfloat16)

    for m in range(4):
        heads = pl.ds(group_of(m, core, z, zp) * 3, 3)
        messages[m][0] = rotate(k_ref[heads])
        messages[m][1] = v_ref[heads]
        messages[m][2] = rotate(q_ref[heads])

    heads = pl.ds(za * 3, 3)
    rows = lax.broadcasted_iota(jnp.int32, (TEXT, 256), 0)
    source = lax.broadcasted_iota(jnp.int32, (TEXT, 256), 1)
    pick = (source == x * 64 + (rows // 4) * 16 + y * 4 + rows % 4).astype(jnp.float32).astype(jnp.bfloat16)
    tq = tq_ref[heads]
    for out, c in ((own_text, core), (send_text, 1 - core)):
        half = pl.ds(pl.multiple_of(c * 128, 128), 128)
        out[:, :128] = tk_ref[heads, half]
        out[:, 128:256] = tv_ref[heads, half]
        for h in range(3):
            out[h, 256:] = jnp.dot(pick, tq[h], preferred_element_type=jnp.float32).astype(jnp.bfloat16)


def prepare(q, k, v, positions, tq, tk, tv):
    message = jax.ShapeDtypeStruct((3, 3, 64, HD), jnp.bfloat16)
    text = jax.ShapeDtypeStruct((3, PACK, HD), jnp.bfloat16)
    return pl.pallas_call(
        prepare_body,
        out_shape=[message] * 4 + [text] * 2,
        cost_estimate=pl.CostEstimate(flops=50000000, bytes_accessed=3000000, transcendentals=20000),
        compiler_params=pltpu.CompilerParams(vmem_limit_bytes=32 * 1024 * 1024),
        name="prepare",
    )(q, k, v, positions, tq, tk, tv, jnp.asarray(FREQ), jnp.asarray(SWAP, jnp.bfloat16))


def softmax_step(q, k, v, state, live=None):
    s = lax.dot_general(q, k, NT, preferred_element_type=jnp.float32)
    if live is not None:
        s = jnp.where(live(s.shape), s, -jnp.inf)
    peak = jnp.max(s, axis=1, keepdims=True)
    if state is not None:
        acc, top, total = state
        peak = jnp.maximum(top, peak)
    p = jnp.exp2(s * SCALE2 - peak * SCALE2)
    add = jnp.sum(p, axis=1, keepdims=True)
    mixed = jnp.dot(p.astype(jnp.bfloat16), v, preferred_element_type=jnp.float32)
    if state is None:
        return mixed, peak, add
    alpha = jnp.exp2((top - peak) * SCALE2)
    return acc * alpha + mixed, peak, total * alpha + add


def over_parts(q, parts, state, most=1024):
    for part in parts:
        pieces, tokens = part.shape[0], part.shape[3]
        step = max(1, most // tokens)
        for i in range(0, pieces, step):
            n = min(step, pieces - i)
            k = part[i : i + n, 0, 0].reshape(n * tokens, HD)
            v = part[i : i + n, 1, 0].reshape(n * tokens, HD)
            state = softmax_step(q, k, v, state)
    return state


def keep(state, acc_ref, stat_ref):
    acc, top, total = state
    acc_ref[0] = acc
    lane = lax.broadcasted_iota(jnp.int32, acc.shape, 1)
    stat_ref[0] = jnp.where(lane < 64, top, total)


def kept(acc_ref, stat_ref):
    stat = stat_ref[0]
    return acc_ref[0], stat[:, :1], stat[:, 64:65]


def first_body(count_ref, m0, m1, m2, m3, mine, theirs, *refs):
    core, z, za, zp, zb = place()
    parts, (q_out, acc_out, stat_out) = refs[:-3], refs[-3:]
    for i, m in enumerate((m0, m1, m2, m3)):
        q_out[0, i * 64 : (i + 1) * 64] = m[0, 0]
    here = core == zp
    text = jnp.where(here, mine[0].astype(jnp.float32), theirs[0, OTHER:].astype(jnp.float32)).astype(jnp.bfloat16)
    q_out[0, OWN:HALF] = text[256:]
    q_out[0, HALF:] = theirs[0, :OTHER]
    q = q_out[0]
    state = over_parts(q, parts, None)
    left = count_ref[0] - core * 128
    live = lambda shape: lax.broadcasted_iota(jnp.int32, shape, 1) < left
    state = softmax_step(q, text[:128], text[128:256], state, live)
    keep(state, acc_out, stat_out)


def next_body(q_ref, acc_ref, stat_ref, *refs):
    parts, (acc_out, stat_out) = refs[:-2], refs[-2:]
    keep(over_parts(q_ref[0], parts, kept(acc_ref, stat_ref)), acc_out, stat_out)


def last_body(q_ref, acc_ref, stat_ref, *refs):
    parts, (acc_out, stat_out, send_out) = refs[:-3], refs[-3:]
    acc, top, total = over_parts(q_ref[0], parts, kept(acc_ref, stat_ref))
    lane = lax.broadcasted_iota(jnp.int32, (HALF, HD), 1)
    acc_out[0] = acc[:HALF]
    stat_out[0] = jnp.where(lane < 64, top[:HALF] * SCALE2, total[:HALF])
    send_out[0, :, :HD] = (acc[OWN:] / total[OWN:]).astype(jnp.bfloat16)
    level = top[OWN:] * SCALE2 + jnp.log2(total[OWN:])
    high = level.astype(jnp.bfloat16).astype(jnp.float32)
    mid = (level - high).astype(jnp.bfloat16).astype(jnp.float32)
    low = level - high - mid
    send_out[0, :, HD:] = jnp.where(lane < 32, high, jnp.where(lane < 64, mid, low)).astype(jnp.bfloat16)


def part_spec(part):
    return pl.BlockSpec((part.shape[0], 2, 1) + part.shape[3:], lambda h, *_: (0, 0, h, 0, 0))


def head_spec(*shape):
    return pl.BlockSpec((1,) + shape, lambda h, *_: (h,) + (0,) * len(shape))


def attend(body, name, parts, extra, extra_specs, outs, prefetch=()):
    keys = sum(p.shape[0] * p.shape[3] for p in parts)
    return pl.pallas_call(
        body,
        out_shape=[jax.ShapeDtypeStruct((3,) + s, t) for s, t in outs],
        grid_spec=pltpu.PrefetchScalarGridSpec(
            num_scalar_prefetch=len(prefetch),
            grid=(3,),
            in_specs=list(extra_specs) + [part_spec(p) for p in parts],
            out_specs=[head_spec(*s) for s, _ in outs],
        ),
        compiler_params=pltpu.CompilerParams(vmem_limit_bytes=40 * 1024 * 1024),
        cost_estimate=pl.CostEstimate(
            flops=12 * QROWS * keys * HD, bytes_accessed=keys * 1536 + 3000000, transcendentals=3 * QROWS * keys
        ),
        name=name,
    )(*prefetch, *extra, *parts)


F32, BF16 = jnp.float32, jnp.bfloat16
STATE = [((QROWS, HD), F32), ((QROWS, HD), F32)]


def merge_body(acc_ref, stat_ref, theirs, *outs):
    def weigh(rows, sent_rows):
        stat = stat_ref[0, rows]
        total = stat[:, 64:65]
        level = stat[:, :1] + jnp.log2(total)
        sent = theirs[0, sent_rows, HD:].astype(F32)
        level2 = sent[:, :1] + sent[:, 32:33] + sent[:, 64:65]
        peak = jnp.maximum(level, level2)
        w1, w2 = jnp.exp2(level - peak), jnp.exp2(level2 - peak)
        inv = 1.0 / (w1 + w2)
        return (acc_ref[0, rows] * (w1 * inv / total) + theirs[0, sent_rows, :HD].astype(F32) * (w2 * inv)).astype(BF16)

    video = weigh(slice(0, OWN), slice(TEXT, HALF))
    text = weigh(slice(OWN, HALF), slice(0, TEXT))
    for m in range(4):
        outs[m][0, :64] = video[m * 64 : (m + 1) * 64]
        outs[m][0, 64:] = text


def merge(acc, stat, theirs):
    return pl.pallas_call(
        merge_body,
        out_shape=[jax.ShapeDtypeStruct((3, 64 + TEXT, HD), BF16)] * 4,
        grid=(3,),
        in_specs=[head_spec(HALF, HD), head_spec(HALF, HD), head_spec(HALF, 2 * HD)],
        out_specs=[head_spec(64 + TEXT, HD)] * 4,
        name="merge",
    )(acc, stat, theirs)


def finish_body(*refs):
    messages, (video, text) = refs[:4], refs[4:]
    core, z, za, zp, zb = place()
    for m in range(4):
        group = group_of(m, core, z, zp)
        video[pl.ds(group * 3, 3)] = messages[m][:, :64]

        @pl.when(group // 2 == zb)
        def _():
            for h in range(3):
                rows = messages[m][h, 64:].astype(F32)
                own = jnp.zeros((4, HD), F32)
                for i in range(4):
                    own = jnp.where(za * 2 + zp == i, rows[4 * i : 4 * i + 4], own)
                text[lax.rem(group, 2) * 3 + h] = own.astype(BF16)


def finish(messages):
    return pl.pallas_call(
        finish_body,
        out_shape=[jax.ShapeDtypeStruct((12, 64, HD), BF16), jax.ShapeDtypeStruct((6, 4, HD), BF16)],
        name="finish",
    )(*messages)


def ring(block, axis):
    right, left = shift(block, axis, 1), shift(block, axis, -1)
    return right, left


def local(video_q, video_k, video_v, positions, text_q, text_k, text_v, text_count):
    flat = lambda a: jnp.transpose(a, (1, 0, 2))
    *out, own_text, send_text = prepare(
        flat(video_q), flat(video_k), flat(video_v), positions, flat(text_q), flat(text_k), flat(text_v)
    )
    m = [z_send(out[i], i) for i in range(4)]

    block_a = jnp.concatenate([m[0][:2], m[1][:2]], axis=2)
    right_a, left_a = ring(block_a, "x")
    block_b = jnp.concatenate([m[2][:2], m[3][:2]], axis=2)
    right_b, left_b = ring(block_b, "y")
    theirs = other_core(jnp.concatenate([m[0][2], m[1][2], m[2][2], m[3][2], send_text], axis=1))
    far_a = [shift(right_a[0], "x", 1), shift(left_a[1], "x", -1)]
    far_b = [shift(right_b[0], "y", 1), shift(left_b[1], "y", -1)]
    line_a = jnp.stack([block_a, right_a, left_a, jnp.stack(far_a)])
    line_b = jnp.stack([block_b, right_b, left_b, jnp.stack(far_b)])
    line_a, line_b, theirs = lax.optimization_barrier((line_a, line_b, theirs))

    right_a, left_a = ring(line_a, "y")
    right_b, left_b = ring(line_b, "x")
    q_specs = [pl.BlockSpec((1, 1, 64, HD), lambda h, *_: (2, h, 0, 0))] * 4
    q, acc, stat = attend(
        first_body,
        "attend_first",
        [line_a, line_b],
        [*m, own_text, theirs],
        q_specs + [head_spec(PACK, HD), head_spec(OTHER + PACK, HD)],
        [((QROWS, HD), BF16)] + STATE,
        prefetch=(text_count,),
    )
    right_a, left_a, right_b, left_b, acc, stat = lax.optimization_barrier(
        (right_a, left_a, right_b, left_b, acc, stat)
    )
    far = [shift(right_a[:2], "y", 1), shift(left_a[2:], "y", -1), shift(right_b[:2], "x", 1), shift(left_b[2:], "x", -1)]
    specs = [head_spec(QROWS, HD)] * 3
    acc, stat = attend(next_body, "attend_next", [right_a, left_a, right_b, left_b], [q, acc, stat], specs, STATE)
    acc, stat, send = attend(
        last_body,
        "attend_last",
        far,
        [q, acc, stat],
        specs,
        [((HALF, HD), F32), ((HALF, HD), F32), ((HALF, 2 * HD), BF16)],
    )
    done = merge(acc, stat, other_core(send))
    video, text = finish([z_return(done[i], i) for i in range(4)])
    return flat(video), flat(text)


def solution(mesh):
    fine = Mesh(mesh.devices.reshape(2, 4, 2, 2, 4, 2), ("grp", "x", "za", "zp", "y", "zb"))
    ctx = ("x", "za", "zp", "y")
    tokens = P(ctx + ("zb",), "grp", None)
    text = P(None, ("grp", "zb"), None)
    return jax.shard_map(
        local,
        mesh=fine,
        in_specs=(tokens, tokens, tokens, P(None, ctx + ("zb",)), text, text, text, P()),
        out_specs=(tokens, P(ctx, ("grp", "zb"), None)),
        check_vma=False,
    )
```

```python
import functools
import math

import jax
import jax.numpy as jnp
import numpy as np
from jax import lax
from jax.experimental import pallas as pl
from jax.experimental.pallas import tpu as pltpu
from jax.sharding import Mesh
from jax.sharding import PartitionSpec as P

THETA = 256.0
HD = 128
SCALE2 = math.log2(math.e) / math.sqrt(HD)
NT = (((1,), (1,)), ((), ()))
TN = (((0,), (0,)), ((), ()))

MOVES = (0, 1, -1, 2)
ZAXES = ("za", "zp", "zb")
VIDEO, TEXT, STATS = 256, 16, 16
SITE = VIDEO + TEXT
SHARE = 64
TILE = 2 * SITE
VMEM = 60 * 1024 * 1024
F32, BF16 = jnp.float32, jnp.bfloat16


def rotary_constants():
    freq = np.zeros((3, HD), np.float32)
    swap = np.zeros((HD, HD), np.float32)
    band_t = HD // 8
    band_h = (HD - band_t) // 2
    offset = 0
    for axis, band in enumerate((band_t, band_h, HD - band_t - band_h)):
        half = band // 2
        f = THETA ** (-2.0 * np.arange(half) / band)
        freq[axis, offset : offset + half] = f
        freq[axis, offset + half : offset + band] = f
        for i in range(half):
            swap[offset + half + i, offset + i] = -1.0
            swap[offset + i, offset + half + i] = 1.0
        offset += band
    return freq, swap


FREQ, SWAP = rotary_constants()


def shift(v, axis, step):
    return lax.ppermute(v, axis, [(i, (i + step) % 4) for i in range(4)])


def z_shift(v, step):
    line = lambda z: (z % 4) * 2 + z // 4
    return lax.ppermute(v, ZAXES, [(line(z), line((z + step) % 8)) for z in range(8)])


def to_far_half(v):
    return lax.ppermute(v, ("y", "zb"), [(y * 2 + y // 2, y * 2 + 1 - y // 2) for y in range(4)])


def group_of(m):
    return lax.rem(lax.axis_index("y") + (MOVES[m] + 4), 4)


def whole(*shape):
    return pl.BlockSpec(shape, lambda i: (0,) * len(shape))


def prepare_body(q_ref, k_ref, v_ref, pos_ref, tq_ref, tk_ref, tv_ref, freq_ref, swap_ref, *outs):
    x, y = lax.axis_index("x"), lax.axis_index("y")
    low = lax.axis_index("za") * 2 + lax.axis_index("zp")
    kv_out, q_out, text_out, text_q_out = outs[:4], outs[4:8], outs[8], outs[9]
    angles = lax.dot_general(
        pos_ref[...].astype(F32), freq_ref[...], TN, precision=lax.Precision.HIGHEST, preferred_element_type=F32
    )
    cos, sin = jnp.cos(angles), jnp.sin(angles)
    swap = swap_ref[...]

    def rotate(block):
        swapped = jnp.dot(block.reshape(3 * 64, HD), swap, preferred_element_type=F32)
        return (block.astype(F32) * cos + swapped.reshape(3, 64, HD) * sin).astype(BF16)

    for m in range(4):
        heads = pl.ds(group_of(m) * 3, 3)
        kv_out[m][0] = rotate(k_ref[heads])
        kv_out[m][1] = v_ref[heads]
        q_out[m][...] = rotate(q_ref[heads])

    heads = pl.ds(lax.rem(y, 2) * 3, 3)
    share = pl.ds(pl.multiple_of(x * SHARE, SHARE), SHARE)
    text_out[:, :SHARE] = tk_ref[heads, share]
    text_out[:, SHARE:] = tv_ref[heads, share]
    text_q_out[...] = tq_ref[heads, pl.ds(pl.multiple_of(x * 64 + low * TEXT, TEXT), TEXT)]


def prepare(q, k, v, positions, tq, tk, tv):
    outs = [(2, 3, 64, HD)] * 4 + [(3, 64, HD)] * 4 + [(3, 2 * SHARE, HD), (3, TEXT, HD)]
    args = (q, k, v, positions, tq, tk, tv, jnp.asarray(FREQ), jnp.asarray(SWAP, BF16))
    return pl.pallas_call(
        prepare_body,
        out_shape=[jax.ShapeDtypeStruct(o, BF16) for o in outs],
        grid=(1,),
        in_specs=[whole(*a.shape) for a in args],
        out_specs=[whole(*o) for o in outs],
        cost_estimate=pl.CostEstimate(flops=50000000, bytes_accessed=3000000, transcendentals=20000),
        compiler_params=pltpu.CompilerParams(vmem_limit_bytes=VMEM),
        name="prepare",
    )(*args)


def softmax_step(q, k, v, state, live=None):
    s = lax.dot_general(q, k, NT, preferred_element_type=F32)
    if live is not None:
        s = jnp.where(live(s.shape), s, -jnp.inf)
    peak = jnp.max(s, axis=1, keepdims=True)
    if state is not None:
        acc, top, total = state
        peak = jnp.maximum(top, peak)
    p = jnp.exp2(s * SCALE2 - peak * SCALE2)
    add = jnp.sum(p, axis=1, keepdims=True)
    mixed = jnp.dot(p.astype(BF16), v, preferred_element_type=F32)
    if state is None:
        return mixed, peak, add
    alpha = jnp.exp2((top - peak) * SCALE2)
    return acc * alpha + mixed, peak, total * alpha + add


def over_parts(q, refs, state):
    keys = jnp.concatenate([r[...].reshape(-1, HD) for r in refs[0::2]], axis=0)
    values = jnp.concatenate([r[...].reshape(-1, HD) for r in refs[1::2]], axis=0)
    return softmax_step(q, keys, values, state)


def keep(state, acc_ref, stat_ref):
    acc, top, total = state
    acc_ref[0] = acc
    lane = lax.broadcasted_iota(jnp.int32, acc.shape, 1)
    stat_ref[0] = jnp.where(lane < 64, top, total)


def kept(acc_ref, stat_ref):
    stat = stat_ref[0]
    first = lax.broadcasted_iota(jnp.int32, stat.shape, 1) < 64
    top = jnp.max(jnp.where(first, stat, -jnp.inf), axis=1, keepdims=True)
    return acc_ref[0], top, jnp.max(jnp.where(first, 0.0, stat), axis=1, keepdims=True)


def first_body(count_ref, q_ref, mine, sent, *refs):
    parts, (acc_out, stat_out) = refs[:-2], refs[-2:]
    q = q_ref[0]
    state = over_parts(q, parts, None)
    here = lax.axis_index("y") // 2 == lax.axis_index("zb")
    text = jnp.where(here, mine[0].astype(F32), sent[0].astype(F32)).astype(BF16)
    left = count_ref[0] - lax.axis_index("x") * SHARE
    live = lambda shape: lax.broadcasted_iota(jnp.int32, shape, 1) < left
    keep(softmax_step(q, text[:SHARE], text[SHARE:], state, live), acc_out, stat_out)


def next_body(q_ref, acc_ref, stat_ref, *refs):
    parts, (acc_out, stat_out) = refs[:-2], refs[-2:]
    keep(over_parts(q_ref[0], parts, kept(acc_ref, stat_ref)), acc_out, stat_out)


def diagonal(n):
    return lax.broadcasted_iota(jnp.int32, (n, HD), 0) == lax.broadcasted_iota(jnp.int32, (n, HD), 1)


def pack_level(level):
    place = lax.broadcasted_iota(jnp.int32, (STATS, HD), 0)
    block = jnp.zeros((STATS, HD), F32)
    for t in range(0, SITE, HD):
        n = min(HD, SITE - t)
        row = jnp.sum(jnp.where(diagonal(n), level[t : t + n], 0.0), axis=0, keepdims=True)
        for i in range(3):
            part = row.astype(BF16).astype(F32)
            block = jnp.where(place == t // HD * 3 + i, part, block)
            row = row - part
    return block.astype(BF16)


def unpack_level(block, t, n):
    i = t // HD * 3
    rows = block.astype(F32)
    row = rows[i : i + 1] + rows[i + 1 : i + 2] + rows[i + 2 : i + 3]
    return jnp.sum(jnp.where(diagonal(n), row, 0.0), axis=1, keepdims=True)


def last_body(q_ref, acc_ref, stat_ref, *refs):
    parts, outs = refs[:-4], refs[-4:]
    acc, top, total = over_parts(q_ref[0], parts, kept(acc_ref, stat_ref))
    mean = (acc / total).astype(BF16)
    level = top * SCALE2 + jnp.log2(total)
    for tile in range(2):

        @pl.when(pl.program_id(1) == tile)
        def _():
            for i in range(2):
                out = outs[tile * 2 + i]
                out[0, :SITE] = mean[i * SITE : (i + 1) * SITE]
                out[0, SITE:] = pack_level(level[i * SITE : (i + 1) * SITE])


def head_spec(*shape):
    return pl.BlockSpec((1,) + shape, lambda h, t, *_: (h,) + (0,) * len(shape))


TILE_SPEC = pl.BlockSpec((1, TILE, HD), lambda h, t, *_: (h, t, 0))


def key_specs(part):
    if part.ndim == 3:
        return [head_spec(*part.shape[1:])]
    return [pl.BlockSpec((1, 1) + part.shape[2:], lambda h, t, *_, i=i: (i, h, 0, 0)) for i in range(2)]


def attend(body, name, parts, extra, extra_specs, outs, out_specs, prefetch=()):
    keys = sum(p.shape[-2] for p in parts)
    specs, args = list(extra_specs), list(extra)
    for p in parts:
        new = key_specs(p)
        specs += new
        args += [p] * len(new)
    return pl.pallas_call(
        body,
        out_shape=[jax.ShapeDtypeStruct((3,) + s, t) for s, t in outs],
        grid_spec=pltpu.PrefetchScalarGridSpec(
            num_scalar_prefetch=len(prefetch), grid=(3, 2), in_specs=specs, out_specs=out_specs
        ),
        compiler_params=pltpu.CompilerParams(vmem_limit_bytes=VMEM),
        cost_estimate=pl.CostEstimate(
            flops=24 * TILE * keys * HD, bytes_accessed=keys * 1536 + 6000000, transcendentals=6 * TILE * keys
        ),
        name=name,
    )(*prefetch, *args)


STATE = [((2 * TILE, HD), F32)] * 2


def merge_body(*refs):
    sites, outs = refs[:4], refs[4:]
    for t in range(0, SITE, HD):
        n = min(HD, SITE - t)
        levels = [unpack_level(s[0, SITE:], t, n) for s in sites]
        peak = functools.reduce(jnp.maximum, levels)
        weights = [jnp.exp2(level - peak) for level in levels]
        mixed = sum(w * s[0, t : t + n].astype(F32) for w, s in zip(weights, sites))
        mixed = (mixed / sum(weights)).astype(BF16)
        if t < VIDEO:
            for i in range(0, n, 64):
                outs[(t + i) // 64][0, :64] = mixed[i : i + 64]
        else:
            for out in outs:
                out[0, 64:] = mixed


def merge(sites):
    spec = lambda rows: pl.BlockSpec((1, rows, HD), lambda h: (h, 0, 0))
    return pl.pallas_call(
        merge_body,
        out_shape=[jax.ShapeDtypeStruct((3, 64 + TEXT, HD), BF16)] * 4,
        grid=(3,),
        in_specs=[spec(SITE + STATS)] * 4,
        out_specs=[spec(64 + TEXT)] * 4,
        compiler_params=pltpu.CompilerParams(vmem_limit_bytes=VMEM),
        name="merge",
    )(*sites)


def finish_body(*refs):
    messages, (video, text) = refs[:4], refs[4:]
    y, zb = lax.axis_index("y"), lax.axis_index("zb")
    for m in range(4):
        group = group_of(m)
        video[pl.ds(group * 3, 3)] = messages[m][:, :64]

        @pl.when(group // 2 == zb)
        def _():
            for h in range(3):
                rows = messages[m][h, 64:].astype(F32)
                own = jnp.zeros((4, HD), F32)
                for i in range(4):
                    own = jnp.where(y == i, rows[4 * i : 4 * i + 4], own)
                text[lax.rem(group, 2) * 3 + h] = own.astype(BF16)


def finish(messages):
    return pl.pallas_call(
        finish_body,
        out_shape=[jax.ShapeDtypeStruct((12, 64, HD), BF16), jax.ShapeDtypeStruct((6, 4, HD), BF16)],
        grid=(1,),
        in_specs=[whole(3, 64 + TEXT, HD)] * 4,
        out_specs=[whole(12, 64, HD), whole(6, 4, HD)],
        compiler_params=pltpu.CompilerParams(vmem_limit_bytes=VMEM),
        name="finish",
    )(*messages)


def local(video_q, video_k, video_v, positions, text_q, text_k, text_v, text_count):
    flat = lambda a: jnp.transpose(a, (1, 0, 2))
    out = prepare(flat(video_q), flat(video_k), flat(video_v), positions, flat(text_q), flat(text_k), flat(text_v))
    kv, q, text, text_rows = out[:4], out[4:8], out[8], out[9]
    along_y = lambda v, m: shift(v, "y", MOVES[m])
    block = jnp.concatenate([kv[0]] + [along_y(kv[m], m) for m in range(1, 4)], axis=2)
    right, left = z_shift(block, 1), z_shift(block, -1)
    text_sent = to_far_half(text)
    site = jnp.concatenate([q[0]] + [along_y(q[m], m) for m in range(1, 4)] + [text_rows], axis=1)
    queries = jnp.concatenate([site] + [shift(site, "x", -d) for d in MOVES[1:]], axis=1)

    right2, left2 = z_shift(right, 1), z_shift(left, -1)
    pack = head_spec(2 * SHARE, HD)
    acc, stat = attend(
        first_body,
        "attend_first",
        [block, right, left],
        [queries, text, text_sent],
        [TILE_SPEC, pack, pack],
        STATE,
        [TILE_SPEC] * 2,
        prefetch=(text_count,),
    )
    right3, left3 = z_shift(right2, 1), z_shift(left2, -1)
    specs = [TILE_SPEC] * 3
    acc, stat = attend(next_body, "attend_2", [right2, left2], [queries, acc, stat], specs, STATE, [TILE_SPEC] * 2)
    far_k, far_v = z_shift(right3[0], 1), z_shift(left3[1], -1)
    acc, stat = attend(next_body, "attend_3", [right3, left3], [queries, acc, stat], specs, STATE, [TILE_SPEC] * 2)
    sites = attend(
        last_body,
        "attend_last",
        [far_k, far_v],
        [queries, acc, stat],
        specs,
        [((SITE + STATS, HD), BF16)] * 4,
        [head_spec(SITE + STATS, HD)] * 4,
    )
    done = merge([sites[0]] + [shift(sites[i], "x", MOVES[i]) for i in range(1, 4)])
    video, text = finish([done[0]] + [shift(done[m], "y", -MOVES[m]) for m in range(1, 4)])
    return flat(video), flat(text)


def solution(mesh):
    fine = Mesh(mesh.devices.reshape(2, 4, 2, 2, 4, 2), ("grp", "x", "za", "zp", "y", "zb"))
    ctx = ("x", "za", "zp", "y")
    tokens = P(ctx + ("zb",), "grp", None)
    text = P(None, ("grp", "zb"), None)
    return jax.shard_map(
        local,
        mesh=fine,
        in_specs=(tokens, tokens, tokens, P(None, ctx + ("zb",)), text, text, text, P()),
        out_specs=(tokens, P(ctx, ("grp", "zb"), None)),
        check_vma=False,
    )
```

```python
import functools
import math

import jax
import jax.numpy as jnp
import numpy as np
from jax import lax
from jax.experimental import pallas as pl
from jax.experimental.pallas import tpu as pltpu
from jax.sharding import Mesh
from jax.sharding import PartitionSpec as P

THETA = 256.0
HD = 128
SCALE2 = math.log2(math.e) / math.sqrt(HD)
NT = (((1,), (1,)), ((), ()))
TN = (((0,), (0,)), ((), ()))

MOVES = (0, 1, -1, 2)
ZAXES = ("za", "zp", "zb")
VIDEO, TEXT, STATS = 256, 16, 16
SITE = VIDEO + TEXT
SHARE = 64
TILE = 2 * SITE
VMEM = 60 * 1024 * 1024
F32, BF16 = jnp.float32, jnp.bfloat16


def rotary_constants():
    freq = np.zeros((3, HD), np.float32)
    swap = np.zeros((HD, HD), np.float32)
    band_t = HD // 8
    band_h = (HD - band_t) // 2
    offset = 0
    for axis, band in enumerate((band_t, band_h, HD - band_t - band_h)):
        half = band // 2
        f = THETA ** (-2.0 * np.arange(half) / band)
        freq[axis, offset : offset + half] = f
        freq[axis, offset + half : offset + band] = f
        for i in range(half):
            swap[offset + half + i, offset + i] = -1.0
            swap[offset + i, offset + half + i] = 1.0
        offset += band
    return freq, swap


FREQ, SWAP = rotary_constants()


def shift(v, axis, step):
    return lax.ppermute(v, axis, [(i, (i + step) % 4) for i in range(4)])


def z_shift(v, step):
    line = lambda z: (z % 4) * 2 + z // 4
    return lax.ppermute(v, ZAXES, [(line(z), line((z + step) % 8)) for z in range(8)])


def to_far_half(v):
    return lax.ppermute(v, ("y", "zb"), [(y * 2 + y // 2, y * 2 + 1 - y // 2) for y in range(4)])


def group_of(m):
    return lax.rem(lax.axis_index("y") + (MOVES[m] + 4), 4)


def whole(*shape):
    return pl.BlockSpec(shape, lambda i: (0,) * len(shape))


def prepare_body(q_ref, k_ref, v_ref, pos_ref, tq_ref, tk_ref, tv_ref, freq_ref, swap_ref, *outs):
    x, y = lax.axis_index("x"), lax.axis_index("y")
    low = lax.axis_index("za") * 2 + lax.axis_index("zp")
    messages, text_out, text_q_out = outs[:4], outs[4], outs[5]
    angles = lax.dot_general(
        pos_ref[...].astype(F32), freq_ref[...], TN, precision=lax.Precision.HIGHEST, preferred_element_type=F32
    )
    cos, sin = jnp.cos(angles), jnp.sin(angles)
    swap = swap_ref[...]

    def rotate(block):
        swapped = jnp.dot(block.reshape(3 * 64, HD), swap, preferred_element_type=F32)
        return (block.astype(F32) * cos + swapped.reshape(3, 64, HD) * sin).astype(BF16)

    for m in range(4):
        heads = pl.ds(group_of(m) * 3, 3)
        messages[m][0] = rotate(k_ref[heads])
        messages[m][1] = v_ref[heads]
        messages[m][2] = rotate(q_ref[heads])

    heads = pl.ds(lax.rem(y, 2) * 3, 3)
    share = pl.ds(pl.multiple_of(x * SHARE, SHARE), SHARE)
    text_out[:, :SHARE] = tk_ref[heads, share]
    text_out[:, SHARE:] = tv_ref[heads, share]
    text_q_out[...] = tq_ref[heads, pl.ds(pl.multiple_of(x * 64 + low * TEXT, TEXT), TEXT)]


def prepare(q, k, v, positions, tq, tk, tv):
    outs = [(3, 3, 64, HD)] * 4 + [(3, 2 * SHARE, HD), (3, TEXT, HD)]
    args = (q, k, v, positions, tq, tk, tv, jnp.asarray(FREQ), jnp.asarray(SWAP, BF16))
    return pl.pallas_call(
        prepare_body,
        out_shape=[jax.ShapeDtypeStruct(o, BF16) for o in outs],
        grid=(1,),
        in_specs=[whole(*a.shape) for a in args],
        out_specs=[whole(*o) for o in outs],
        cost_estimate=pl.CostEstimate(flops=50000000, bytes_accessed=3000000, transcendentals=20000),
        compiler_params=pltpu.CompilerParams(vmem_limit_bytes=VMEM),
        name="prepare",
    )(*args)


def widen(v, n):
    return jnp.concatenate([v] * (n // HD), axis=1) if n >= HD else v[:, :n]


def softmax_step(q, k, v, state, live=None):
    s = lax.dot_general(q, k, NT, preferred_element_type=F32)
    if live is not None:
        s = jnp.where(live(s.shape), s, -jnp.inf)
    lanes = (s.shape[0], HD)
    peak = jnp.broadcast_to(jnp.max(s, axis=1, keepdims=True) * SCALE2, lanes)
    if state is not None:
        acc, top, total = state
        peak = jnp.maximum(top, peak)
    p = jnp.exp2(s * SCALE2 - widen(peak, s.shape[1]))
    add = jnp.broadcast_to(jnp.sum(p, axis=1, keepdims=True), lanes)
    mixed = jnp.dot(p.astype(BF16), v, preferred_element_type=F32)
    if state is None:
        return mixed, peak, add
    alpha = jnp.exp2(top - peak)
    return acc * alpha + mixed, peak, total * alpha + add


def over_parts(q, refs, state):
    keys = jnp.concatenate([r[...].reshape(-1, HD) for r in refs[0::2]], axis=0)
    values = jnp.concatenate([r[...].reshape(-1, HD) for r in refs[1::2]], axis=0)
    return softmax_step(q, keys, values, state)


def rows_here():
    return pl.program_id(0), pl.ds(pl.multiple_of(pl.program_id(1) * TILE, 16), TILE)


def keep(state, refs):
    for value, ref in zip(state, refs):
        ref[rows_here()] = value


def kept(refs):
    return tuple(ref[rows_here()] for ref in refs)


def first_body(count_ref, q_ref, mine, sent, *refs):
    parts, outs = refs[:-3], refs[-3:]
    q = q_ref[0]
    state = over_parts(q, parts, None)
    here = lax.axis_index("y") // 2 == lax.axis_index("zb")
    text = jnp.where(here, mine[0].astype(F32), sent[0].astype(F32)).astype(BF16)
    left = count_ref[0] - lax.axis_index("x") * SHARE
    live = lambda shape: lax.broadcasted_iota(jnp.int32, shape, 1) < left
    keep(softmax_step(q, text[:SHARE], text[SHARE:], state, live), outs)


def next_body(q_ref, acc_ref, top_ref, total_ref, *refs):
    parts, outs = refs[:-3], refs[-3:]
    keep(over_parts(q_ref[0], parts, kept((acc_ref, top_ref, total_ref))), outs)


def pack_level(level):
    blocks = []
    for t in range(0, SITE, HD):
        n = min(HD, SITE - t)
        lane = lax.broadcasted_iota(jnp.int32, (n, HD), 1)
        rest, parts = level[t : t + n], jnp.zeros((n, HD), F32)
        for i in range(3):
            part = rest.astype(BF16).astype(F32)
            parts = jnp.where(lane == t // HD * 3 + i, part, parts)
            rest = rest - part
        unit = (lane == lax.broadcasted_iota(jnp.int32, (n, HD), 0)).astype(F32).astype(BF16)
        blocks.append(lax.dot_general(parts.astype(BF16), unit, TN, preferred_element_type=F32))
    return sum(blocks)[:STATS].astype(BF16)


def unpack_level(block, t, n):
    first = t // HD * 3
    place = lax.broadcasted_iota(jnp.int32, (STATS, HD), 0)
    pick = ((place >= first) & (place < first + 3)).astype(F32).astype(BF16)
    return lax.dot_general(block, pick, TN, preferred_element_type=F32)[:n]


def last_body(q_ref, acc_ref, top_ref, total_ref, *refs):
    parts, outs = refs[:-4], refs[-4:]
    acc, top, total = over_parts(q_ref[0], parts, kept((acc_ref, top_ref, total_ref)))
    mean = (acc / total).astype(BF16)
    level = top + jnp.log2(total)
    for tile in range(2):

        @pl.when(pl.program_id(1) == tile)
        def _():
            for i in range(2):
                out = outs[tile * 2 + i]
                out[0, :SITE] = mean[i * SITE : (i + 1) * SITE]
                out[0, SITE:] = pack_level(level[i * SITE : (i + 1) * SITE])


def head_spec(*shape):
    return pl.BlockSpec((1,) + shape, lambda h, t, *_: (h,) + (0,) * len(shape))


TILE_SPEC = pl.BlockSpec((1, TILE, HD), lambda h, t, *_: (h, t, 0))


def key_specs(part):
    if part.ndim == 3:
        return [head_spec(*part.shape[1:])]
    return [pl.BlockSpec((1, 1) + part.shape[2:], lambda h, t, *_, i=i: (i, h, 0, 0)) for i in range(2)]


def attend(body, name, parts, extra, extra_specs, outs, out_specs, prefetch=()):
    keys = sum(p.shape[-2] for p in parts)
    specs, args = list(extra_specs), list(extra)
    for p in parts:
        new = key_specs(p)
        specs += new
        args += [p] * len(new)
    return pl.pallas_call(
        body,
        out_shape=[jax.ShapeDtypeStruct((3,) + s, t) for s, t in outs],
        grid_spec=pltpu.PrefetchScalarGridSpec(
            num_scalar_prefetch=len(prefetch), grid=(3, 2), in_specs=specs, out_specs=out_specs
        ),
        compiler_params=pltpu.CompilerParams(vmem_limit_bytes=VMEM // 2),
        cost_estimate=pl.CostEstimate(
            flops=24 * TILE * keys * HD, bytes_accessed=keys * 1536 + 6000000, transcendentals=6 * TILE * keys
        ),
        name=name,
    )(*prefetch, *args)


STATE = [((2 * TILE, HD), F32)] * 3
STATE_SPECS = [pl.BlockSpec(memory_space=pltpu.VMEM)] * 3


def merge_body(*refs):
    sites, outs = refs[:4], refs[4:]
    for t in range(0, SITE, HD):
        n = min(HD, SITE - t)
        levels = [unpack_level(s[0, SITE:], t, n) for s in sites]
        peak = functools.reduce(jnp.maximum, levels)
        weights = [jnp.exp2(level - peak) for level in levels]
        mixed = sum(w * s[0, t : t + n].astype(F32) for w, s in zip(weights, sites))
        mixed = (mixed / sum(weights)).astype(BF16)
        if t < VIDEO:
            for i in range(0, n, 64):
                outs[(t + i) // 64][0, :64] = mixed[i : i + 64]
        else:
            for out in outs:
                out[0, 64:] = mixed


def merge(sites):
    spec = lambda rows: pl.BlockSpec((1, rows, HD), lambda h: (h, 0, 0))
    return pl.pallas_call(
        merge_body,
        out_shape=[jax.ShapeDtypeStruct((3, 64 + TEXT, HD), BF16)] * 4,
        grid=(3,),
        in_specs=[spec(SITE + STATS)] * 4,
        out_specs=[spec(64 + TEXT)] * 4,
        compiler_params=pltpu.CompilerParams(vmem_limit_bytes=VMEM),
        name="merge",
    )(*sites)


def finish_body(*refs):
    messages, (video, text) = refs[:4], refs[4:]
    y, zb = lax.axis_index("y"), lax.axis_index("zb")
    for m in range(4):
        group = group_of(m)
        video[pl.ds(group * 3, 3)] = messages[m][:, :64]

        @pl.when(group // 2 == zb)
        def _():
            for h in range(3):
                rows = messages[m][h, 64:].astype(F32)
                own = jnp.zeros((4, HD), F32)
                for i in range(4):
                    own = jnp.where(y == i, rows[4 * i : 4 * i + 4], own)
                text[lax.rem(group, 2) * 3 + h] = own.astype(BF16)


def finish(messages):
    return pl.pallas_call(
        finish_body,
        out_shape=[jax.ShapeDtypeStruct((12, 64, HD), BF16), jax.ShapeDtypeStruct((6, 4, HD), BF16)],
        grid=(1,),
        in_specs=[whole(3, 64 + TEXT, HD)] * 4,
        out_specs=[whole(12, 64, HD), whole(6, 4, HD)],
        compiler_params=pltpu.CompilerParams(vmem_limit_bytes=VMEM),
        name="finish",
    )(*messages)


def local(video_q, video_k, video_v, positions, text_q, text_k, text_v, text_count):
    flat = lambda a: jnp.transpose(a, (1, 0, 2))
    out = prepare(flat(video_q), flat(video_k), flat(video_v), positions, flat(text_q), flat(text_k), flat(text_v))
    own, text, text_rows = out[:4], out[4], out[5]
    text_sent = to_far_half(text)
    m = [own[0]] + [shift(own[i], "y", MOVES[i]) for i in range(1, 4)]
    block = jnp.concatenate([v[:2] for v in m], axis=2)
    block, text_sent = lax.optimization_barrier((block, text_sent))
    right, left = z_shift(block, 1), z_shift(block, -1)
    site = jnp.concatenate([v[2] for v in m] + [text_rows], axis=1)
    queries = jnp.concatenate([site] + [shift(site, "x", -d) for d in MOVES[1:]], axis=1)

    right2, left2 = z_shift(right, 1), z_shift(left, -1)
    pack = head_spec(2 * SHARE, HD)
    state = attend(
        first_body,
        "attend_first",
        [block, right, left],
        [queries, text, text_sent],
        [TILE_SPEC, pack, pack],
        STATE,
        STATE_SPECS,
        prefetch=(text_count,),
    )
    right2, left2, *state = lax.optimization_barrier((right2, left2, *state))
    right3, left3 = z_shift(right2, 1), z_shift(left2, -1)
    specs = [TILE_SPEC] + STATE_SPECS
    state = attend(next_body, "attend_2", [right2, left2], [queries, *state], specs, STATE, STATE_SPECS)
    right3, left3, *state = lax.optimization_barrier((right3, left3, *state))
    far_k, far_v = z_shift(right3[0], 1), z_shift(left3[1], -1)
    state = attend(next_body, "attend_3", [right3, left3], [queries, *state], specs, STATE, STATE_SPECS)
    sites = attend(
        last_body,
        "attend_last",
        [far_k, far_v],
        [queries, *state],
        specs,
        [((SITE + STATS, HD), BF16)] * 4,
        [head_spec(SITE + STATS, HD)] * 4,
    )
    done = merge([sites[0]] + [shift(sites[i], "x", MOVES[i]) for i in range(1, 4)])
    video, text = finish([done[0]] + [shift(done[m], "y", -MOVES[m]) for m in range(1, 4)])
    return flat(video), flat(text)


def solution(mesh):
    fine = Mesh(mesh.devices.reshape(2, 4, 2, 2, 4, 2), ("grp", "x", "za", "zp", "y", "zb"))
    ctx = ("x", "za", "zp", "y")
    tokens = P(ctx + ("zb",), "grp", None)
    text = P(None, ("grp", "zb"), None)
    return jax.shard_map(
        local,
        mesh=fine,
        in_specs=(tokens, tokens, tokens, P(None, ctx + ("zb",)), text, text, text, P()),
        out_specs=(tokens, P(ctx, ("grp", "zb"), None)),
        check_vma=False,
    )
```

```python
import functools
import math

import jax
import jax.numpy as jnp
import numpy as np
from jax import lax
from jax.experimental import pallas as pl
from jax.experimental.pallas import tpu as pltpu
from jax.sharding import Mesh
from jax.sharding import PartitionSpec as P

THETA = 256.0
HD = 128
SCALE2 = math.log2(math.e) / math.sqrt(HD)
NT = (((1,), (1,)), ((), ()))
TN = (((0,), (0,)), ((), ()))

MOVES = (0, 1, -1, 2)
ZAXES = ("za", "zp", "zb")
VIDEO, TEXT, STATS = 256, 16, 16
SITE = VIDEO + TEXT
OFFSETS = (0, -1, 1, -2, 2, -3, 3, 4)
TILE = 2 * SITE
VMEM = 63 * 1024 * 1024
F32, BF16 = jnp.float32, jnp.bfloat16


def rotary_constants():
    freq = np.zeros((3, HD), np.float32)
    swap = np.zeros((HD, HD), np.float32)
    band_t = HD // 8
    band_h = (HD - band_t) // 2
    offset = 0
    for axis, band in enumerate((band_t, band_h, HD - band_t - band_h)):
        half = band // 2
        f = THETA ** (-2.0 * np.arange(half) / band)
        freq[axis, offset : offset + half] = f
        freq[axis, offset + half : offset + band] = f
        for i in range(half):
            swap[offset + half + i, offset + i] = -1.0
            swap[offset + i, offset + half + i] = 1.0
        offset += band
    return freq, swap


FREQ, SWAP = rotary_constants()


def shift(v, axis, step):
    return lax.ppermute(v, axis, [(i, (i + step) % 4) for i in range(4)])


def z_shift(v, step):
    line = lambda z: (z % 4) * 2 + z // 4
    return lax.ppermute(v, ZAXES, [(line(z), line((z + step) % 8)) for z in range(8)])


def group_of(m):
    return lax.rem(lax.axis_index("y") + (MOVES[m] + 4), 4)


def whole(*shape):
    return pl.BlockSpec(shape, lambda i: (0,) * len(shape))


def prepare_body(q_ref, k_ref, v_ref, pos_ref, tq_ref, tk_ref, tv_ref, freq_ref, swap_ref, *outs):
    x, y = lax.axis_index("x"), lax.axis_index("y")
    low = lax.axis_index("za") * 2 + lax.axis_index("zp")
    messages, text_out, text_q_out = outs[:4], outs[4], outs[5]
    angles = lax.dot_general(
        pos_ref[...].astype(F32), freq_ref[...], TN, precision=lax.Precision.HIGHEST, preferred_element_type=F32
    )
    cos, sin = jnp.cos(angles), jnp.sin(angles)
    swap = swap_ref[...]

    def rotate(block):
        swapped = jnp.dot(block.reshape(3 * 64, HD), swap, preferred_element_type=F32)
        return (block.astype(F32) * cos + swapped.reshape(3, 64, HD) * sin).astype(BF16)

    for m in range(4):
        heads = pl.ds(group_of(m) * 3, 3)
        messages[m][0] = rotate(k_ref[heads])
        messages[m][1] = v_ref[heads]
        messages[m][2] = rotate(q_ref[heads])

    heads = pl.ds(lax.rem(y, 2) * 3, 3)
    share = pl.ds(pl.multiple_of(x * 64 + low * TEXT, TEXT), TEXT)
    text_out[0] = tk_ref[heads, share]
    text_out[1] = tv_ref[heads, share]
    text_q_out[...] = tq_ref[heads, share]


def prepare(q, k, v, positions, tq, tk, tv):
    outs = [(3, 3, 64, HD)] * 4 + [(2, 3, TEXT, HD), (3, TEXT, HD)]
    args = (q, k, v, positions, tq, tk, tv, jnp.asarray(FREQ), jnp.asarray(SWAP, BF16))
    return pl.pallas_call(
        prepare_body,
        out_shape=[jax.ShapeDtypeStruct(o, BF16) for o in outs],
        grid=(1,),
        in_specs=[whole(*a.shape) for a in args],
        out_specs=[whole(*o) for o in outs],
        cost_estimate=pl.CostEstimate(flops=50000000, bytes_accessed=3000000, transcendentals=20000),
        compiler_params=pltpu.CompilerParams(vmem_limit_bytes=VMEM),
        name="prepare",
    )(*args)


def widen(v, n):
    return jnp.concatenate([v] * (n // HD), axis=1) if n >= HD else v[:, :n]


def softmax_step(q, k, v, state, live=None):
    s = lax.dot_general(q, k, NT, preferred_element_type=F32)
    if live is not None:
        s = jnp.where(live(s.shape), s, -jnp.inf)
    lanes = (s.shape[0], HD)
    peak = jnp.broadcast_to(jnp.max(s, axis=1, keepdims=True) * SCALE2, lanes)
    if state is not None:
        acc, top, total = state
        peak = jnp.maximum(top, peak)
    p = jnp.exp2(s * SCALE2 - widen(peak, s.shape[1]))
    add = jnp.broadcast_to(jnp.sum(p, axis=1, keepdims=True), lanes)
    mixed = jnp.dot(p.astype(BF16), v, preferred_element_type=F32)
    if state is None:
        return mixed, peak, add
    alpha = jnp.exp2(top - peak)
    return acc * alpha + mixed, peak, total * alpha + add


def joined(refs):
    keys = jnp.concatenate([r[...].reshape(-1, HD) for r in refs[0::2]], axis=0)
    return keys, jnp.concatenate([r[...].reshape(-1, HD) for r in refs[1::2]], axis=0)


TILES = [slice(0, TILE), slice(TILE, 2 * TILE)]


def keep(state, refs, rows):
    for value, ref in zip(state, refs):
        ref[pl.program_id(0), rows] = value


def kept(refs, rows):
    return tuple(ref[pl.program_id(0), rows] for ref in refs)


def first_body(q_ref, *refs):
    parts, outs = refs[:-3], refs[-3:]
    keys, values = joined(parts)
    for rows in TILES:
        keep(softmax_step(q_ref[0, rows], keys, values, None), outs, rows)


def next_body(q_ref, acc_ref, top_ref, total_ref, *refs):
    parts, outs = refs[:-3], refs[-3:]
    keys, values = joined(parts)
    for rows in TILES:
        state = kept((acc_ref, top_ref, total_ref), rows)
        keep(softmax_step(q_ref[0, rows], keys, values, state), outs, rows)


def pack_level(level):
    blocks = []
    for t in range(0, SITE, HD):
        n = min(HD, SITE - t)
        lane = lax.broadcasted_iota(jnp.int32, (n, HD), 1)
        rest, parts = level[t : t + n], jnp.zeros((n, HD), F32)
        for i in range(3):
            part = rest.astype(BF16).astype(F32)
            parts = jnp.where(lane == t // HD * 3 + i, part, parts)
            rest = rest - part
        unit = (lane == lax.broadcasted_iota(jnp.int32, (n, HD), 0)).astype(F32).astype(BF16)
        blocks.append(lax.dot_general(parts.astype(BF16), unit, TN, preferred_element_type=F32))
    return sum(blocks)[:STATS].astype(BF16)


def unpack_level(block, t, n):
    first = t // HD * 3
    place = lax.broadcasted_iota(jnp.int32, (STATS, HD), 0)
    pick = ((place >= first) & (place < first + 3)).astype(F32).astype(BF16)
    return lax.dot_general(block, pick, TN, preferred_element_type=F32)[:n]


def live_text(count, shape):
    z = lax.axis_index("zb") * 4 + lax.axis_index("za") * 2 + lax.axis_index("zp")
    lane = lax.broadcasted_iota(jnp.int32, shape, 1)
    source = jnp.zeros(shape, jnp.int32)
    for i, offset in enumerate(OFFSETS):
        source = jnp.where(lane // TEXT == i, lax.rem(z + (offset + 8), 8), source)
    index = lax.axis_index("x") * 64 + source % 4 * TEXT + lane % TEXT
    return (source // 4 == lax.axis_index("y") // 2) & (index < count)


def last_body(count_ref, q_ref, acc_ref, top_ref, total_ref, *refs):
    parts, text, outs = refs[:2], refs[2:-4], refs[-4:]
    keys, values = joined(parts)
    text_keys, text_values = joined(text)
    live = lambda shape: live_text(count_ref[0], shape)
    for tile, rows in enumerate(TILES):
        state = kept((acc_ref, top_ref, total_ref), rows)
        state = softmax_step(q_ref[0, rows], text_keys, text_values, state, live)
        acc, top, total = softmax_step(q_ref[0, rows], keys, values, state)
        mean = (acc / total).astype(BF16)
        level = top + jnp.log2(total)
        for i in range(2):
            out = outs[tile * 2 + i]
            out[0, :SITE] = mean[i * SITE : (i + 1) * SITE]
            out[0, SITE:] = pack_level(level[i * SITE : (i + 1) * SITE])


def head_spec(*shape):
    return pl.BlockSpec((1,) + shape, lambda h, *_: (h,) + (0,) * len(shape))


TILE_SPEC = head_spec(2 * TILE, HD)


def key_specs(part, rows=VIDEO, at=0):
    if part.ndim == 3:
        return [pl.BlockSpec((1, rows, HD), lambda h, *_: (h, at, 0))]
    return [pl.BlockSpec((1, 1, rows, HD), lambda h, *_, i=i: (i, h, at, 0)) for i in range(2)]


def attend(body, name, parts, extra, extra_specs, outs, out_specs, prefetch=(), texts=()):
    keys = VIDEO * len(parts)
    specs, args = list(extra_specs), list(extra)
    for p in parts:
        new = key_specs(p)
        specs += new
        args += [p] * len(new)
    for p in texts:
        new = key_specs(p, TEXT, VIDEO // TEXT)
        specs += new
        args += [p] * len(new)
    return pl.pallas_call(
        body,
        out_shape=[jax.ShapeDtypeStruct((3,) + s, t) for s, t in outs],
        grid_spec=pltpu.PrefetchScalarGridSpec(
            num_scalar_prefetch=len(prefetch), grid=(3,), in_specs=specs, out_specs=out_specs
        ),
        compiler_params=pltpu.CompilerParams(vmem_limit_bytes=VMEM // 2),
        cost_estimate=pl.CostEstimate(
            flops=24 * TILE * keys * HD, bytes_accessed=keys * 1536 + 6000000, transcendentals=6 * TILE * keys
        ),
        name=name,
    )(*prefetch, *args)


STATE = [((2 * TILE, HD), F32)] * 3
STATE_SPECS = [pl.BlockSpec(memory_space=pltpu.VMEM)] * 3


def merge_body(*refs):
    sites, outs = refs[:4], refs[4:]
    for h in range(3):
        for t in range(0, SITE, HD):
            n = min(HD, SITE - t)
            levels = [unpack_level(s[h, SITE:], t, n) for s in sites]
            peak = functools.reduce(jnp.maximum, levels)
            weights = [jnp.exp2(level - peak) for level in levels]
            mixed = sum(w * s[h, t : t + n].astype(F32) for w, s in zip(weights, sites))
            mixed = (mixed / sum(weights)).astype(BF16)
            if t < VIDEO:
                for i in range(0, n, 64):
                    outs[(t + i) // 64][h, :64] = mixed[i : i + 64]
            else:
                for out in outs:
                    out[h, 64:] = mixed


def merge(sites):
    return pl.pallas_call(
        merge_body,
        out_shape=[jax.ShapeDtypeStruct((3, 64 + TEXT, HD), BF16)] * 4,
        grid=(1,),
        in_specs=[whole(3, SITE + STATS, HD)] * 4,
        out_specs=[whole(3, 64 + TEXT, HD)] * 4,
        compiler_params=pltpu.CompilerParams(vmem_limit_bytes=VMEM),
        name="merge",
    )(*sites)


def finish_body(*refs):
    messages, (video, text) = refs[:4], refs[4:]
    y, zb = lax.axis_index("y"), lax.axis_index("zb")
    for m in range(4):
        group = group_of(m)
        video[pl.ds(group * 3, 3)] = messages[m][:, :64]

        @pl.when(group // 2 == zb)
        def _():
            for h in range(3):
                rows = messages[m][h, 64:].astype(F32)
                own = jnp.zeros((4, HD), F32)
                for i in range(4):
                    own = jnp.where(y == i, rows[4 * i : 4 * i + 4], own)
                text[lax.rem(group, 2) * 3 + h] = own.astype(BF16)


def finish(messages):
    return pl.pallas_call(
        finish_body,
        out_shape=[jax.ShapeDtypeStruct((12, 64, HD), BF16), jax.ShapeDtypeStruct((6, 4, HD), BF16)],
        grid=(1,),
        in_specs=[whole(3, 64 + TEXT, HD)] * 4,
        out_specs=[whole(12, 64, HD), whole(6, 4, HD)],
        compiler_params=pltpu.CompilerParams(vmem_limit_bytes=VMEM),
        name="finish",
    )(*messages)


def local(video_q, video_k, video_v, positions, text_q, text_k, text_v, text_count):
    flat = lambda a: jnp.transpose(a, (1, 0, 2))
    out = prepare(flat(video_q), flat(video_k), flat(video_v), positions, flat(text_q), flat(text_k), flat(text_v))
    own, text, text_rows = out[:4], out[4], out[5]
    m = [own[0]] + [shift(own[i], "y", MOVES[i]) for i in range(1, 4)]
    block = jnp.concatenate([v[:2] for v in m] + [text], axis=2)
    right, left = z_shift(block, 1), z_shift(block, -1)
    site = jnp.concatenate([v[2] for v in m] + [text_rows], axis=1)
    queries = jnp.concatenate([site] + [shift(site, "x", -d) for d in MOVES[1:]], axis=1)

    right2, left2 = z_shift(right, 1), z_shift(left, -1)
    state = attend(
        first_body,
        "attend_first",
        [block, right],
        [queries],
        [TILE_SPEC],
        STATE,
        STATE_SPECS,
    )
    right2, left2, *state = lax.optimization_barrier((right2, left2, *state))
    right3, left3 = z_shift(right2, 1), z_shift(left2, -1)
    specs = [TILE_SPEC] + STATE_SPECS
    state = attend(next_body, "attend_2", [left, right2, left2], [queries, *state], specs, STATE, STATE_SPECS)
    right3, left3, *state = lax.optimization_barrier((right3, left3, *state))
    far_k, far_v = z_shift(right3[0], 1), z_shift(left3[1], -1)
    state = attend(next_body, "attend_3", [right3, left3], [queries, *state], specs, STATE, STATE_SPECS)
    sites = attend(
        last_body,
        "attend_last",
        [far_k, far_v],
        [queries, *state],
        specs,
        [((SITE + STATS, HD), BF16)] * 4,
        [head_spec(SITE + STATS, HD)] * 4,
        prefetch=(text_count,),
        texts=[block, right, left, right2, left2, right3, left3, far_k, far_v],
    )
    done = merge([sites[0]] + [shift(sites[i], "x", MOVES[i]) for i in range(1, 4)])
    video, text = finish([done[0]] + [shift(done[m], "y", -MOVES[m]) for m in range(1, 4)])
    return flat(video), flat(text)


def solution(mesh):
    fine = Mesh(mesh.devices.reshape(2, 4, 2, 2, 4, 2), ("grp", "x", "za", "zp", "y", "zb"))
    ctx = ("x", "za", "zp", "y")
    tokens = P(ctx + ("zb",), "grp", None)
    text = P(None, ("grp", "zb"), None)
    return jax.shard_map(
        local,
        mesh=fine,
        in_specs=(tokens, tokens, tokens, P(None, ctx + ("zb",)), text, text, text, P()),
        out_specs=(tokens, P(ctx, ("grp", "zb"), None)),
        check_vma=False,
    )
```

```python
import functools
import math

import jax
import jax.numpy as jnp
import numpy as np
from jax import lax
from jax.experimental import pallas as pl
from jax.experimental.pallas import tpu as pltpu
from jax.sharding import Mesh
from jax.sharding import PartitionSpec as P

THETA = 256.0
HD = 128
SCALE2 = math.log2(math.e) / math.sqrt(HD)
NT = (((1,), (1,)), ((), ()))
TN = (((0,), (0,)), ((), ()))

MOVES = (0, 1, -1, 2)
ZAXES = ("za", "zp", "zb")
VIDEO, TEXT, STATS = 256, 16, 16
SITE = VIDEO + TEXT
OFFSETS = (0, -1, 1, -2, 2, -3, 3, 4)
TILE = 2 * SITE
VMEM = 63 * 1024 * 1024
F32, BF16 = jnp.float32, jnp.bfloat16


def rotary_constants():
    freq = np.zeros((3, HD), np.float32)
    swap = np.zeros((HD, HD), np.float32)
    band_t = HD // 8
    band_h = (HD - band_t) // 2
    offset = 0
    for axis, band in enumerate((band_t, band_h, HD - band_t - band_h)):
        half = band // 2
        f = THETA ** (-2.0 * np.arange(half) / band)
        freq[axis, offset : offset + half] = f
        freq[axis, offset + half : offset + band] = f
        for i in range(half):
            swap[offset + half + i, offset + i] = -1.0
            swap[offset + i, offset + half + i] = 1.0
        offset += band
    return freq, swap


FREQ, SWAP = rotary_constants()


def shift(v, axis, step):
    return lax.ppermute(v, axis, [(i, (i + step) % 4) for i in range(4)])


def z_shift(v, step):
    line = lambda z: (z % 4) * 2 + z // 4
    return lax.ppermute(v, ZAXES, [(line(z), line((z + step) % 8)) for z in range(8)])


def group_of(m):
    return lax.rem(lax.axis_index("y") + (MOVES[m] + 4), 4)


def whole(*shape):
    return pl.BlockSpec(shape, lambda i: (0,) * len(shape))


IN_VMEM = pl.BlockSpec(memory_space=pltpu.VMEM)


def prepare_body(q_ref, k_ref, v_ref, pos_ref, tq_ref, tk_ref, tv_ref, freq_ref, swap_ref, *outs):
    x, y = lax.axis_index("x"), lax.axis_index("y")
    low = lax.axis_index("za") * 2 + lax.axis_index("zp")
    messages, text_out, text_q_out = outs[:4], outs[4], outs[5]
    angles = lax.dot_general(
        pos_ref[...].astype(F32), freq_ref[...], TN, precision=lax.Precision.HIGHEST, preferred_element_type=F32
    )
    cos, sin = jnp.cos(angles), jnp.sin(angles)
    swap = swap_ref[...]

    def rotate(block):
        swapped = jnp.dot(block.reshape(3 * 64, HD), swap, preferred_element_type=F32)
        return (block.astype(F32) * cos + swapped.reshape(3, 64, HD) * sin).astype(BF16)

    for m in range(4):
        heads = pl.ds(group_of(m) * 3, 3)
        messages[m][0] = rotate(k_ref[heads])
        messages[m][1] = v_ref[heads]
        messages[m][2] = rotate(q_ref[heads])

    heads = pl.ds(lax.rem(y, 2) * 3, 3)
    share = pl.ds(pl.multiple_of(x * 64 + low * TEXT, TEXT), TEXT)
    text_out[0] = tk_ref[heads, share]
    text_out[1] = tv_ref[heads, share]
    text_q_out[...] = tq_ref[heads, share]


def prepare(q, k, v, positions, tq, tk, tv):
    outs = [(3, 3, 64, HD)] * 4 + [(2, 3, TEXT, HD), (3, TEXT, HD)]
    args = (q, k, v, positions, tq, tk, tv, jnp.asarray(FREQ), jnp.asarray(SWAP, BF16))
    return pl.pallas_call(
        prepare_body,
        out_shape=[jax.ShapeDtypeStruct(o, BF16) for o in outs],
        grid=(1,),
        in_specs=[whole(*a.shape) for a in args],
        out_specs=[whole(*o) for o in outs],
        cost_estimate=pl.CostEstimate(flops=50000000, bytes_accessed=3000000, transcendentals=20000),
        compiler_params=pltpu.CompilerParams(vmem_limit_bytes=VMEM),
        name="prepare",
    )(*args)


def widen(v, n):
    return jnp.concatenate([v] * (n // HD), axis=1) if n >= HD else v[:, :n]


def softmax_step(q, k, v, state, live=None):
    s = lax.dot_general(q, k, NT, preferred_element_type=F32)
    if live is not None:
        s = jnp.where(live(s.shape), s, -jnp.inf)
    lanes = (s.shape[0], HD)
    peak = jnp.broadcast_to(jnp.max(s, axis=1, keepdims=True) * SCALE2, lanes)
    if state is not None:
        acc, top, total = state
        peak = jnp.maximum(top, peak)
    p = jnp.exp2(s * SCALE2 - widen(peak, s.shape[1]))
    add = jnp.broadcast_to(jnp.sum(p, axis=1, keepdims=True), lanes)
    mixed = jnp.dot(p.astype(BF16), v, preferred_element_type=F32)
    if state is None:
        return mixed, peak, add
    alpha = jnp.exp2(top - peak)
    return acc * alpha + mixed, peak, total * alpha + add


def joined(refs):
    keys = jnp.concatenate([r[...].reshape(-1, HD) for r in refs[0::2]], axis=0)
    return keys, jnp.concatenate([r[...].reshape(-1, HD) for r in refs[1::2]], axis=0)


TILES = [slice(0, TILE), slice(TILE, 2 * TILE)]


def keep(state, refs, rows):
    for value, ref in zip(state, refs):
        ref[pl.program_id(0), rows] = value


def kept(refs, rows):
    return tuple(ref[pl.program_id(0), rows] for ref in refs)


def first_body(q_ref, *refs):
    parts, outs = refs[:-3], refs[-3:]
    keys, values = joined(parts)
    for rows in TILES:
        keep(softmax_step(q_ref[0, rows], keys, values, None), outs, rows)


def next_body(q_ref, acc_ref, top_ref, total_ref, *refs):
    parts, outs = refs[:-3], refs[-3:]
    keys, values = joined(parts)
    for rows in TILES:
        state = kept((acc_ref, top_ref, total_ref), rows)
        keep(softmax_step(q_ref[0, rows], keys, values, state), outs, rows)


def pack_level(level):
    blocks = []
    for t in range(0, SITE, HD):
        n = min(HD, SITE - t)
        lane = lax.broadcasted_iota(jnp.int32, (n, HD), 1)
        rest, parts = level[t : t + n], jnp.zeros((n, HD), F32)
        for i in range(3):
            part = rest.astype(BF16).astype(F32)
            parts = jnp.where(lane == t // HD * 3 + i, part, parts)
            rest = rest - part
        unit = (lane == lax.broadcasted_iota(jnp.int32, (n, HD), 0)).astype(F32).astype(BF16)
        blocks.append(lax.dot_general(parts.astype(BF16), unit, TN, preferred_element_type=F32))
    return sum(blocks)[:STATS].astype(BF16)


def unpack_level(block, t, n):
    first = t // HD * 3
    place = lax.broadcasted_iota(jnp.int32, (STATS, HD), 0)
    pick = ((place >= first) & (place < first + 3)).astype(F32).astype(BF16)
    return lax.dot_general(block, pick, TN, preferred_element_type=F32)[:n]


def live_text(count, shape):
    z = lax.axis_index("zb") * 4 + lax.axis_index("za") * 2 + lax.axis_index("zp")
    lane = lax.broadcasted_iota(jnp.int32, shape, 1)
    source = jnp.zeros(shape, jnp.int32)
    for i, offset in enumerate(OFFSETS):
        source = jnp.where(lane // TEXT == i, lax.rem(z + (offset + 8), 8), source)
    index = lax.axis_index("x") * 64 + source % 4 * TEXT + lane % TEXT
    return (source // 4 == lax.axis_index("y") // 2) & (index < count)


def last_body(count_ref, q_ref, acc_ref, top_ref, total_ref, *refs):
    parts, text, outs = refs[:2], refs[2:-4], refs[-4:]
    keys, values = joined(parts)
    text_keys, text_values = joined(text)
    live = lambda shape: live_text(count_ref[0], shape)
    for tile, rows in enumerate(TILES):
        state = kept((acc_ref, top_ref, total_ref), rows)
        state = softmax_step(q_ref[0, rows], text_keys, text_values, state, live)
        acc, top, total = softmax_step(q_ref[0, rows], keys, values, state)
        mean = (acc / total).astype(BF16)
        level = top + jnp.log2(total)
        for i in range(2):
            out = outs[tile * 2 + i]
            out[0, :SITE] = mean[i * SITE : (i + 1) * SITE]
            out[0, SITE:] = pack_level(level[i * SITE : (i + 1) * SITE])


def head_spec(*shape):
    return pl.BlockSpec((1,) + shape, lambda h, *_: (h,) + (0,) * len(shape))


TILE_SPEC = head_spec(2 * TILE, HD)


def key_specs(part, rows=VIDEO, at=0):
    if part.ndim == 3:
        return [pl.BlockSpec((1, rows, HD), lambda h, *_: (h, at, 0))]
    return [pl.BlockSpec((1, 1, rows, HD), lambda h, *_, i=i: (i, h, at, 0)) for i in range(2)]


def attend(body, name, parts, extra, extra_specs, outs, out_specs, prefetch=(), texts=()):
    keys = VIDEO * len(parts)
    specs, args = list(extra_specs), list(extra)
    for p in parts:
        new = key_specs(p)
        specs += new
        args += [p] * len(new)
    for p in texts:
        new = key_specs(p, TEXT, VIDEO // TEXT)
        specs += new
        args += [p] * len(new)
    return pl.pallas_call(
        body,
        out_shape=[jax.ShapeDtypeStruct((3,) + s, t) for s, t in outs],
        grid_spec=pltpu.PrefetchScalarGridSpec(
            num_scalar_prefetch=len(prefetch), grid=(3,), in_specs=specs, out_specs=out_specs
        ),
        compiler_params=pltpu.CompilerParams(vmem_limit_bytes=VMEM // 2),
        cost_estimate=pl.CostEstimate(
            flops=24 * TILE * keys * HD, bytes_accessed=keys * 1536 + 6000000, transcendentals=6 * TILE * keys
        ),
        name=name,
    )(*prefetch, *args)


STATE = [((2 * TILE, HD), F32)] * 3
STATE_SPECS = [IN_VMEM] * 3


def merge_body(*refs):
    sites, outs = refs[:4], refs[4:]
    for h in range(3):
        for t in range(0, SITE, HD):
            n = min(HD, SITE - t)
            levels = [unpack_level(s[h, SITE:], t, n) for s in sites]
            peak = functools.reduce(jnp.maximum, levels)
            weights = [jnp.exp2(level - peak) for level in levels]
            mixed = sum(w * s[h, t : t + n].astype(F32) for w, s in zip(weights, sites))
            mixed = (mixed / sum(weights)).astype(BF16)
            if t < VIDEO:
                for i in range(0, n, 64):
                    outs[(t + i) // 64][h, :64] = mixed[i : i + 64]
            else:
                for out in outs:
                    out[h, 64:] = mixed


def merge(sites):
    return pl.pallas_call(
        merge_body,
        out_shape=[jax.ShapeDtypeStruct((3, 64 + TEXT, HD), BF16)] * 4,
        grid=(1,),
        in_specs=[IN_VMEM] * 4,
        out_specs=[IN_VMEM] * 4,
        compiler_params=pltpu.CompilerParams(vmem_limit_bytes=VMEM // 2),
        name="merge",
    )(*sites)


def finish_body(*refs):
    messages, (video, text) = refs[:4], refs[4:]
    y, zb = lax.axis_index("y"), lax.axis_index("zb")
    for m in range(4):
        group = group_of(m)
        video[pl.ds(group * 3, 3)] = messages[m][:, :64]

        @pl.when(group // 2 == zb)
        def _():
            for h in range(3):
                rows = messages[m][h, 64:].astype(F32)
                own = jnp.zeros((4, HD), F32)
                for i in range(4):
                    own = jnp.where(y == i, rows[4 * i : 4 * i + 4], own)
                text[lax.rem(group, 2) * 3 + h] = own.astype(BF16)


def finish(messages):
    return pl.pallas_call(
        finish_body,
        out_shape=[jax.ShapeDtypeStruct((12, 64, HD), BF16), jax.ShapeDtypeStruct((6, 4, HD), BF16)],
        grid=(1,),
        in_specs=[IN_VMEM] * 4,
        out_specs=[whole(12, 64, HD), whole(6, 4, HD)],
        compiler_params=pltpu.CompilerParams(vmem_limit_bytes=VMEM // 2),
        name="finish",
    )(*messages)


def local(video_q, video_k, video_v, positions, text_q, text_k, text_v, text_count):
    flat = lambda a: jnp.transpose(a, (1, 0, 2))
    out = prepare(flat(video_q), flat(video_k), flat(video_v), positions, flat(text_q), flat(text_k), flat(text_v))
    own, text, text_rows = out[:4], out[4], out[5]
    m = [own[0]] + [shift(own[i], "y", MOVES[i]) for i in range(1, 4)]
    block = jnp.concatenate([v[:2] for v in m] + [text], axis=2)
    right, left = z_shift(block, 1), z_shift(block, -1)
    site = jnp.concatenate([v[2] for v in m] + [text_rows], axis=1)
    queries = jnp.concatenate([site] + [shift(site, "x", -d) for d in MOVES[1:]], axis=1)

    right2, left2 = z_shift(right, 1), z_shift(left, -1)
    state = attend(
        first_body,
        "attend_first",
        [block, right],
        [queries],
        [TILE_SPEC],
        STATE,
        STATE_SPECS,
    )
    right2, left2, *state = lax.optimization_barrier((right2, left2, *state))
    right3, left3 = z_shift(right2, 1), z_shift(left2, -1)
    specs = [TILE_SPEC] + STATE_SPECS
    state = attend(next_body, "attend_2", [left, right2, left2], [queries, *state], specs, STATE, STATE_SPECS)
    right3, left3, *state = lax.optimization_barrier((right3, left3, *state))
    far_k, far_v = z_shift(right3[0], 1), z_shift(left3[1], -1)
    state = attend(next_body, "attend_3", [right3, left3], [queries, *state], specs, STATE, STATE_SPECS)
    sites = attend(
        last_body,
        "attend_last",
        [far_k, far_v],
        [queries, *state],
        specs,
        [((SITE + STATS, HD), BF16)] * 4,
        [head_spec(SITE + STATS, HD)] * 4,
        prefetch=(text_count,),
        texts=[block, right, left, right2, left2, right3, left3, far_k, far_v],
    )
    done = merge([sites[0]] + [shift(sites[i], "x", MOVES[i]) for i in range(1, 4)])
    video, text = finish([done[0]] + [shift(done[m], "y", -MOVES[m]) for m in range(1, 4)])
    return flat(video), flat(text)


def solution(mesh):
    fine = Mesh(mesh.devices.reshape(2, 4, 2, 2, 4, 2), ("grp", "x", "za", "zp", "y", "zb"))
    ctx = ("x", "za", "zp", "y")
    tokens = P(ctx + ("zb",), "grp", None)
    text = P(None, ("grp", "zb"), None)
    return jax.shard_map(
        local,
        mesh=fine,
        in_specs=(tokens, tokens, tokens, P(None, ctx + ("zb",)), text, text, text, P()),
        out_specs=(tokens, P(ctx, ("grp", "zb"), None)),
        check_vma=False,
    )
```

```python
import functools
import math

import jax
import jax.numpy as jnp
import numpy as np
from jax import lax
from jax.experimental import pallas as pl
from jax.experimental.pallas import tpu as pltpu
from jax.sharding import Mesh
from jax.sharding import PartitionSpec as P

THETA = 256.0
HD = 128
SCALE2 = math.log2(math.e) / math.sqrt(HD)
NT = (((1,), (1,)), ((), ()))
TN = (((0,), (0,)), ((), ()))

MOVES = (0, 1, -1, 2)
ZAXES = ("za", "zp", "zb")
VIDEO, TEXT, STATS = 256, 16, 16
SITE = VIDEO + TEXT
OFFSETS = (0, -1, 1, -2, 2, -3, 3, 4)
TILE = 2 * SITE
VMEM = 63 * 1024 * 1024
F32, BF16 = jnp.float32, jnp.bfloat16


def rotary_constants():
    freq = np.zeros((3, HD), np.float32)
    swap = np.zeros((HD, HD), np.float32)
    band_t = HD // 8
    band_h = (HD - band_t) // 2
    offset = 0
    for axis, band in enumerate((band_t, band_h, HD - band_t - band_h)):
        half = band // 2
        f = THETA ** (-2.0 * np.arange(half) / band)
        freq[axis, offset : offset + half] = f
        freq[axis, offset + half : offset + band] = f
        for i in range(half):
            swap[offset + half + i, offset + i] = -1.0
            swap[offset + i, offset + half + i] = 1.0
        offset += band
    return freq, swap


FREQ, SWAP = rotary_constants()


def shift(v, axis, step):
    return lax.ppermute(v, axis, [(i, (i + step) % 4) for i in range(4)])


def z_shift(v, step):
    line = lambda z: (z % 4) * 2 + z // 4
    return lax.ppermute(v, ZAXES, [(line(z), line((z + step) % 8)) for z in range(8)])


def group_of(m):
    return lax.rem(lax.axis_index("y") + (MOVES[m] + 4), 4)


def whole(*shape):
    return pl.BlockSpec(shape, lambda i: (0,) * len(shape))


IN_VMEM = pl.BlockSpec(memory_space=pltpu.VMEM)


def prepare_body(q_ref, k_ref, v_ref, pos_ref, tq_ref, tk_ref, tv_ref, freq_ref, swap_ref, *outs):
    x, y = lax.axis_index("x"), lax.axis_index("y")
    low = lax.axis_index("za") * 2 + lax.axis_index("zp")
    messages, text_out, text_q_out = outs[:4], outs[4], outs[5]
    angles = lax.dot_general(
        pos_ref[...].astype(F32), freq_ref[...], TN, precision=lax.Precision.HIGHEST, preferred_element_type=F32
    )
    cos, sin = jnp.cos(angles), jnp.sin(angles)
    swap = swap_ref[...]

    def rotate(block):
        swapped = jnp.dot(block.reshape(3 * 64, HD), swap, preferred_element_type=F32)
        return (block.astype(F32) * cos + swapped.reshape(3, 64, HD) * sin).astype(BF16)

    for m in range(4):
        heads = pl.ds(group_of(m) * 3, 3)
        messages[m][0] = rotate(k_ref[heads])
        messages[m][1] = v_ref[heads]
        messages[m][2] = rotate(q_ref[heads])

    heads = pl.ds(lax.rem(y, 2) * 3, 3)
    share = pl.ds(pl.multiple_of(x * 64 + low * TEXT, TEXT), TEXT)
    text_out[0] = tk_ref[heads, share]
    text_out[1] = tv_ref[heads, share]
    text_q_out[...] = tq_ref[heads, share]


def prepare(q, k, v, positions, tq, tk, tv):
    outs = [(3, 3, 64, HD)] * 4 + [(2, 3, TEXT, HD), (3, TEXT, HD)]
    args = (q, k, v, positions, tq, tk, tv, jnp.asarray(FREQ), jnp.asarray(SWAP, BF16))
    return pl.pallas_call(
        prepare_body,
        out_shape=[jax.ShapeDtypeStruct(o, BF16) for o in outs],
        grid=(1,),
        in_specs=[whole(*a.shape) for a in args],
        out_specs=[whole(*o) for o in outs],
        cost_estimate=pl.CostEstimate(flops=50000000, bytes_accessed=3000000, transcendentals=20000),
        compiler_params=pltpu.CompilerParams(vmem_limit_bytes=VMEM),
        name="prepare",
    )(*args)


def widen(v, n):
    return jnp.concatenate([v] * (n // HD), axis=1) if n >= HD else v[:, :n]


def softmax_step(q, k, v, state, live=None):
    s = lax.dot_general(q, k, NT, preferred_element_type=F32)
    if live is not None:
        s = s + live
    lanes = (s.shape[0], HD)
    peak = jnp.broadcast_to(jnp.max(s, axis=1, keepdims=True) * SCALE2, lanes)
    if state is not None:
        acc, top, total = state
        peak = jnp.maximum(top, peak)
    p = jnp.exp2(s * SCALE2 - widen(peak, s.shape[1]))
    add = jnp.broadcast_to(jnp.sum(p, axis=1, keepdims=True), lanes)
    mixed = jnp.dot(p.astype(BF16), v, preferred_element_type=F32)
    if state is None:
        return mixed, peak, add
    alpha = jnp.exp2(top - peak)
    return acc * alpha + mixed, peak, total * alpha + add


def joined(refs):
    keys = jnp.concatenate([r[...].reshape(-1, HD) for r in refs[0::2]], axis=0)
    return keys, jnp.concatenate([r[...].reshape(-1, HD) for r in refs[1::2]], axis=0)


TILES = [slice(0, TILE), slice(TILE, 2 * TILE)]


def keep(state, refs, rows):
    for value, ref in zip(state, refs):
        ref[pl.program_id(0), rows] = value


def kept(refs, rows):
    return tuple(ref[pl.program_id(0), rows] for ref in refs)


def first_body(q_ref, *refs):
    parts, outs = refs[:-3], refs[-3:]
    keys, values = joined(parts)
    for rows in TILES:
        keep(softmax_step(q_ref[0, rows], keys, values, None), outs, rows)


def next_body(q_ref, acc_ref, top_ref, total_ref, *refs):
    parts, outs = refs[:-3], refs[-3:]
    keys, values = joined(parts)
    for rows in TILES:
        state = kept((acc_ref, top_ref, total_ref), rows)
        keep(softmax_step(q_ref[0, rows], keys, values, state), outs, rows)


def pack_level(level):
    blocks = []
    for t in range(0, SITE, HD):
        n = min(HD, SITE - t)
        lane = lax.broadcasted_iota(jnp.int32, (n, HD), 1)
        rest, parts = level[t : t + n], jnp.zeros((n, HD), F32)
        for i in range(3):
            part = rest.astype(BF16).astype(F32)
            parts = jnp.where(lane == t // HD * 3 + i, part, parts)
            rest = rest - part
        unit = (lane == lax.broadcasted_iota(jnp.int32, (n, HD), 0)).astype(F32).astype(BF16)
        blocks.append(lax.dot_general(parts.astype(BF16), unit, TN, preferred_element_type=F32))
    return sum(blocks)[:STATS].astype(BF16)


def unpack_level(block, t, n):
    first = t // HD * 3
    place = lax.broadcasted_iota(jnp.int32, (STATS, HD), 0)
    pick = ((place >= first) & (place < first + 3)).astype(F32).astype(BF16)
    return lax.dot_general(block, pick, TN, preferred_element_type=F32)[:n]


def live_text(count, first):
    z = lax.axis_index("zb") * 4 + lax.axis_index("za") * 2 + lax.axis_index("zp")
    all_lanes = lax.broadcasted_iota(jnp.int32, (8, first + TEXT * len(OFFSETS)), 1)
    lane = jnp.maximum(all_lanes - first, 0)
    source = jnp.zeros(lane.shape, jnp.int32)
    for i, offset in enumerate(OFFSETS):
        source = jnp.where(lane // TEXT == i, lax.rem(z + (offset + 8), 8), source)
    index = lax.axis_index("x") * 64 + source % 4 * TEXT + lane % TEXT
    live = (all_lanes < first) | ((source // 4 == lax.axis_index("y") // 2) & (index < count))
    return jnp.where(live, 0.0, -jnp.inf)[:1]


def last_body(count_ref, q_ref, acc_ref, top_ref, total_ref, *refs):
    parts, text, outs = refs[:2], refs[2:-4], refs[-4:]
    keys, values = joined(parts)
    text_keys, text_values = joined(text)
    keys = jnp.concatenate([keys, text_keys], axis=0)
    values = jnp.concatenate([values, text_values], axis=0)
    live = live_text(count_ref[0], VIDEO)
    for tile, rows in enumerate(TILES):
        state = kept((acc_ref, top_ref, total_ref), rows)
        acc, top, total = softmax_step(q_ref[0, rows], keys, values, state, live)
        mean = (acc / total).astype(BF16)
        level = top + jnp.log2(total)
        for i in range(2):
            out = outs[tile * 2 + i]
            out[0, :SITE] = mean[i * SITE : (i + 1) * SITE]
            out[0, SITE:] = pack_level(level[i * SITE : (i + 1) * SITE])


def head_spec(*shape):
    return pl.BlockSpec((1,) + shape, lambda h, *_: (h,) + (0,) * len(shape))


TILE_SPEC = head_spec(2 * TILE, HD)


def key_specs(part, rows=VIDEO, at=0):
    if part.ndim == 3:
        return [pl.BlockSpec((1, rows, HD), lambda h, *_: (h, at, 0))]
    return [pl.BlockSpec((1, 1, rows, HD), lambda h, *_, i=i: (i, h, at, 0)) for i in range(2)]


def attend(body, name, parts, extra, extra_specs, outs, out_specs, prefetch=(), texts=()):
    keys = VIDEO * len(parts)
    specs, args = list(extra_specs), list(extra)
    for p in parts:
        new = key_specs(p)
        specs += new
        args += [p] * len(new)
    for p in texts:
        new = key_specs(p, TEXT, VIDEO // TEXT)
        specs += new
        args += [p] * len(new)
    return pl.pallas_call(
        body,
        out_shape=[jax.ShapeDtypeStruct((3,) + s, t) for s, t in outs],
        grid_spec=pltpu.PrefetchScalarGridSpec(
            num_scalar_prefetch=len(prefetch), grid=(3,), in_specs=specs, out_specs=out_specs
        ),
        compiler_params=pltpu.CompilerParams(vmem_limit_bytes=VMEM // 2),
        cost_estimate=pl.CostEstimate(
            flops=24 * TILE * keys * HD, bytes_accessed=keys * 1536 + 6000000, transcendentals=6 * TILE * keys
        ),
        name=name,
    )(*prefetch, *args)


STATE = [((2 * TILE, HD), F32)] * 3
STATE_SPECS = [IN_VMEM] * 3


def merge_body(*refs):
    sites, outs = refs[:4], refs[4:]
    for h in range(3):
        for t in range(0, SITE, HD):
            n = min(HD, SITE - t)
            levels = [unpack_level(s[h, SITE:], t, n) for s in sites]
            peak = functools.reduce(jnp.maximum, levels)
            weights = [jnp.exp2(level - peak) for level in levels]
            mixed = sum(w * s[h, t : t + n].astype(F32) for w, s in zip(weights, sites))
            mixed = (mixed / sum(weights)).astype(BF16)
            if t < VIDEO:
                for i in range(0, n, 64):
                    outs[(t + i) // 64][h, :64] = mixed[i : i + 64]
            else:
                for out in outs:
                    out[h, 64:] = mixed


def merge(sites):
    return pl.pallas_call(
        merge_body,
        out_shape=[jax.ShapeDtypeStruct((3, 64 + TEXT, HD), BF16)] * 4,
        grid=(1,),
        in_specs=[IN_VMEM] * 4,
        out_specs=[IN_VMEM] * 4,
        compiler_params=pltpu.CompilerParams(vmem_limit_bytes=VMEM // 2),
        name="merge",
    )(*sites)


def finish_body(*refs):
    messages, (video, text) = refs[:4], refs[4:]
    y, zb = lax.axis_index("y"), lax.axis_index("zb")
    for m in range(4):
        group = group_of(m)
        video[pl.ds(group * 3, 3)] = messages[m][:, :64]

        @pl.when(group // 2 == zb)
        def _():
            for h in range(3):
                rows = messages[m][h, 64:].astype(F32)
                own = jnp.zeros((4, HD), F32)
                for i in range(4):
                    own = jnp.where(y == i, rows[4 * i : 4 * i + 4], own)
                text[lax.rem(group, 2) * 3 + h] = own.astype(BF16)


def finish(messages):
    return pl.pallas_call(
        finish_body,
        out_shape=[jax.ShapeDtypeStruct((12, 64, HD), BF16), jax.ShapeDtypeStruct((6, 4, HD), BF16)],
        grid=(1,),
        in_specs=[IN_VMEM] * 4,
        out_specs=[whole(12, 64, HD), whole(6, 4, HD)],
        compiler_params=pltpu.CompilerParams(vmem_limit_bytes=VMEM // 2),
        name="finish",
    )(*messages)


def local(video_q, video_k, video_v, positions, text_q, text_k, text_v, text_count):
    flat = lambda a: jnp.transpose(a, (1, 0, 2))
    out = prepare(flat(video_q), flat(video_k), flat(video_v), positions, flat(text_q), flat(text_k), flat(text_v))
    own, text, text_rows = out[:4], out[4], out[5]
    m = [own[0]] + [shift(own[i], "y", MOVES[i]) for i in range(1, 4)]
    block = jnp.concatenate([v[:2] for v in m] + [text], axis=2)
    right, left = z_shift(block, 1), z_shift(block, -1)
    site = jnp.concatenate([v[2] for v in m] + [text_rows], axis=1)
    queries = jnp.concatenate([site] + [shift(site, "x", -d) for d in MOVES[1:]], axis=1)

    right2, left2 = z_shift(right, 1), z_shift(left, -1)
    state = attend(
        first_body,
        "attend_first",
        [block, right],
        [queries],
        [TILE_SPEC],
        STATE,
        STATE_SPECS,
    )
    right2, left2, *state = lax.optimization_barrier((right2, left2, *state))
    right3, left3 = z_shift(right2, 1), z_shift(left2, -1)
    specs = [TILE_SPEC] + STATE_SPECS
    state = attend(next_body, "attend_2", [left, right2, left2], [queries, *state], specs, STATE, STATE_SPECS)
    right3, left3, *state = lax.optimization_barrier((right3, left3, *state))
    far_k, far_v = z_shift(right3[0], 1), z_shift(left3[1], -1)
    state = attend(next_body, "attend_3", [right3, left3], [queries, *state], specs, STATE, STATE_SPECS)
    sites = attend(
        last_body,
        "attend_last",
        [far_k, far_v],
        [queries, *state],
        specs,
        [((SITE + STATS, HD), BF16)] * 4,
        [head_spec(SITE + STATS, HD)] * 4,
        prefetch=(text_count,),
        texts=[block, right, left, right2, left2, right3, left3, far_k, far_v],
    )
    done = merge([sites[0]] + [shift(sites[i], "x", MOVES[i]) for i in range(1, 4)])
    video, text = finish([done[0]] + [shift(done[m], "y", -MOVES[m]) for m in range(1, 4)])
    return flat(video), flat(text)


def solution(mesh):
    fine = Mesh(mesh.devices.reshape(2, 4, 2, 2, 4, 2), ("grp", "x", "za", "zp", "y", "zb"))
    ctx = ("x", "za", "zp", "y")
    tokens = P(ctx + ("zb",), "grp", None)
    text = P(None, ("grp", "zb"), None)
    return jax.shard_map(
        local,
        mesh=fine,
        in_specs=(tokens, tokens, tokens, P(None, ctx + ("zb",)), text, text, text, P()),
        out_specs=(tokens, P(ctx, ("grp", "zb"), None)),
        check_vma=False,
    )
```

```python
import functools
import math

import jax
import jax.numpy as jnp
import numpy as np
from jax import lax
from jax.experimental import pallas as pl
from jax.experimental.pallas import tpu as pltpu
from jax.sharding import Mesh
from jax.sharding import PartitionSpec as P

THETA = 256.0
HD = 128
SCALE2 = math.log2(math.e) / math.sqrt(HD)
NT = (((1,), (1,)), ((), ()))
TN = (((0,), (0,)), ((), ()))

MOVES = (0, 1, -1, 2)
ZAXES = ("za", "zp", "zb")
VIDEO, TEXT, STATS = 256, 16, 16
SITE = VIDEO + TEXT
OFFSETS = (0, -1, 1, -2, 2, -3, 3, 4)
TILE = 2 * SITE
VMEM = 63 * 1024 * 1024
F32, BF16 = jnp.float32, jnp.bfloat16


def rotary_constants():
    freq = np.zeros((3, HD), np.float32)
    swap = np.zeros((HD, HD), np.float32)
    band_t = HD // 8
    band_h = (HD - band_t) // 2
    offset = 0
    for axis, band in enumerate((band_t, band_h, HD - band_t - band_h)):
        half = band // 2
        f = THETA ** (-2.0 * np.arange(half) / band)
        freq[axis, offset : offset + half] = f
        freq[axis, offset + half : offset + band] = f
        for i in range(half):
            swap[offset + half + i, offset + i] = -1.0
            swap[offset + i, offset + half + i] = 1.0
        offset += band
    return freq, swap


FREQ, SWAP = rotary_constants()


def shift(v, axis, step):
    return lax.ppermute(v, axis, [(i, (i + step) % 4) for i in range(4)])


def z_shift(v, step):
    line = lambda z: (z % 4) * 2 + z // 4
    return lax.ppermute(v, ZAXES, [(line(z), line((z + step) % 8)) for z in range(8)])


def group_of(m):
    return lax.rem(lax.axis_index("y") + (MOVES[m] + 4), 4)


def whole(*shape):
    return pl.BlockSpec(shape, lambda i: (0,) * len(shape))


IN_VMEM = pl.BlockSpec(memory_space=pltpu.VMEM)


def prepare_body(q_ref, k_ref, v_ref, pos_ref, tq_ref, tk_ref, tv_ref, freq_ref, swap_ref, *outs):
    x, y = lax.axis_index("x"), lax.axis_index("y")
    low = lax.axis_index("za") * 2 + lax.axis_index("zp")
    messages, text_out, text_q_out = outs[:4], outs[4], outs[5]
    angles = lax.dot_general(
        pos_ref[...].astype(F32), freq_ref[...], TN, precision=lax.Precision.HIGHEST, preferred_element_type=F32
    )
    cos, sin = jnp.cos(angles), jnp.sin(angles)
    swap = swap_ref[...]

    def rotate(block):
        swapped = jnp.dot(block.reshape(3 * 64, HD), swap, preferred_element_type=F32)
        return (block.astype(F32) * cos + swapped.reshape(3, 64, HD) * sin).astype(BF16)

    for m in range(4):
        heads = pl.ds(group_of(m) * 3, 3)
        messages[m][0] = rotate(k_ref[heads])
        messages[m][1] = v_ref[heads]
        messages[m][2] = rotate(q_ref[heads])

    heads = pl.ds(lax.rem(y, 2) * 3, 3)
    share = pl.ds(pl.multiple_of(x * 64 + low * TEXT, TEXT), TEXT)
    text_out[0] = tk_ref[heads, share]
    text_out[1] = tv_ref[heads, share]
    text_q_out[...] = tq_ref[heads, share]


def prepare(q, k, v, positions, tq, tk, tv):
    outs = [(3, 3, 64, HD)] * 4 + [(2, 3, TEXT, HD), (3, TEXT, HD)]
    args = (q, k, v, positions, tq, tk, tv, jnp.asarray(FREQ), jnp.asarray(SWAP, BF16))
    return pl.pallas_call(
        prepare_body,
        out_shape=[jax.ShapeDtypeStruct(o, BF16) for o in outs],
        grid=(1,),
        in_specs=[whole(*a.shape) for a in args],
        out_specs=[whole(*o) for o in outs],
        cost_estimate=pl.CostEstimate(flops=50000000, bytes_accessed=3000000, transcendentals=20000),
        compiler_params=pltpu.CompilerParams(vmem_limit_bytes=VMEM),
        name="prepare",
    )(*args)


def widen(v, n):
    return jnp.concatenate([v] * (n // HD), axis=1) if n >= HD else v[:, :n]


def softmax_step(q, k, v, state, live=None):
    s = lax.dot_general(q, k, NT, preferred_element_type=F32)
    if live is not None:
        s = s + live
    lanes = (s.shape[0], HD)
    peak = jnp.broadcast_to(jnp.max(s, axis=1, keepdims=True) * SCALE2, lanes)
    if state is not None:
        acc, top, total = state
        peak = jnp.maximum(top, peak)
    p = jnp.exp2(s * SCALE2 - widen(peak, s.shape[1]))
    add = jnp.broadcast_to(jnp.sum(p, axis=1, keepdims=True), lanes)
    mixed = jnp.dot(p.astype(BF16), v, preferred_element_type=F32)
    if state is None:
        return mixed, peak, add
    alpha = jnp.exp2(top - peak)
    return acc * alpha + mixed, peak, total * alpha + add


def joined(refs, skip=TEXT):
    return tuple(jnp.concatenate([r[...].reshape(-1, HD)[skip:] for r in refs[i::2]], axis=0) for i in range(2))


TILES = [slice(0, TILE), slice(TILE, 2 * TILE)]


def keep(state, refs, rows):
    for value, ref in zip(state, refs):
        ref[pl.program_id(0), rows] = value


def kept(refs, rows):
    return tuple(ref[pl.program_id(0), rows] for ref in refs)


def first_body(q_ref, *refs):
    parts, outs = refs[:-3], refs[-3:]
    keys, values = joined(parts)
    for rows in TILES:
        keep(softmax_step(q_ref[0, rows], keys, values, None), outs, rows)


def next_body(q_ref, acc_ref, top_ref, total_ref, *refs):
    parts, outs = refs[:-3], refs[-3:]
    keys, values = joined(parts)
    for rows in TILES:
        state = kept((acc_ref, top_ref, total_ref), rows)
        keep(softmax_step(q_ref[0, rows], keys, values, state), outs, rows)


def pack_level(level):
    blocks = []
    for t in range(0, SITE, HD):
        n = min(HD, SITE - t)
        lane = lax.broadcasted_iota(jnp.int32, (n, HD), 1)
        rest, parts = level[t : t + n], jnp.zeros((n, HD), F32)
        for i in range(3):
            part = rest.astype(BF16).astype(F32)
            parts = jnp.where(lane == t // HD * 3 + i, part, parts)
            rest = rest - part
        unit = (lane == lax.broadcasted_iota(jnp.int32, (n, HD), 0)).astype(F32).astype(BF16)
        blocks.append(lax.dot_general(parts.astype(BF16), unit, TN, preferred_element_type=F32))
    return sum(blocks)[:STATS].astype(BF16)


def unpack_level(block, t, n):
    first = t // HD * 3
    place = lax.broadcasted_iota(jnp.int32, (STATS, HD), 0)
    pick = ((place >= first) & (place < first + 3)).astype(F32).astype(BF16)
    return lax.dot_general(block, pick, TN, preferred_element_type=F32)[:n]


def live_text(count, first):
    z = lax.axis_index("zb") * 4 + lax.axis_index("za") * 2 + lax.axis_index("zp")
    all_lanes = lax.broadcasted_iota(jnp.int32, (8, first + TEXT * len(OFFSETS)), 1)
    lane = jnp.maximum(all_lanes - first, 0)
    source = jnp.zeros(lane.shape, jnp.int32)
    for i, offset in enumerate(OFFSETS):
        source = jnp.where(lane // TEXT == i, lax.rem(z + (offset + 8), 8), source)
    index = lax.axis_index("x") * 64 + source % 4 * TEXT + lane % TEXT
    live = (all_lanes < first) | ((source // 4 == lax.axis_index("y") // 2) & (index < count))
    return jnp.where(live, 0.0, -jnp.inf)[:1]


def last_body(count_ref, q_ref, acc_ref, top_ref, total_ref, *refs):
    parts, text, outs = refs[:2], refs[2:-4], refs[-4:]
    keys, values = joined(parts)
    text_keys, text_values = joined(text, 0)
    keys = jnp.concatenate([keys, text_keys], axis=0)
    values = jnp.concatenate([values, text_values], axis=0)
    live = live_text(count_ref[0], VIDEO)
    for tile, rows in enumerate(TILES):
        state = kept((acc_ref, top_ref, total_ref), rows)
        acc, top, total = softmax_step(q_ref[0, rows], keys, values, state, live)
        mean = (acc / total).astype(BF16)
        level = top + jnp.log2(total)
        for i in range(2):
            out = outs[tile * 2 + i]
            out[0, :SITE] = mean[i * SITE : (i + 1) * SITE]
            out[0, SITE:] = pack_level(level[i * SITE : (i + 1) * SITE])


def head_spec(*shape):
    return pl.BlockSpec((1,) + shape, lambda h, *_: (h,) + (0,) * len(shape))


TILE_SPEC = head_spec(2 * TILE, HD)


def key_specs(part, rows):
    if part.ndim == 3:
        return [head_spec(rows, HD)]
    return [pl.BlockSpec((1, 1, rows, HD), lambda h, *_, i=i: (i, h, 0, 0)) for i in range(2)]


def attend(body, name, parts, extra, extra_specs, outs, out_specs, prefetch=(), texts=()):
    keys = VIDEO * len(parts)
    specs, args = list(extra_specs), list(extra)
    for p in parts:
        new = key_specs(p, VIDEO + TEXT)
        specs += new
        args += [p] * len(new)
    for p in texts:
        new = key_specs(p, TEXT)
        specs += new
        args += [p] * len(new)
    return pl.pallas_call(
        body,
        out_shape=[jax.ShapeDtypeStruct((3,) + s, t) for s, t in outs],
        grid_spec=pltpu.PrefetchScalarGridSpec(
            num_scalar_prefetch=len(prefetch), grid=(3,), in_specs=specs, out_specs=out_specs
        ),
        compiler_params=pltpu.CompilerParams(vmem_limit_bytes=VMEM // 2),
        cost_estimate=pl.CostEstimate(
            flops=24 * TILE * keys * HD, bytes_accessed=keys * 1536 + 6000000, transcendentals=6 * TILE * keys
        ),
        name=name,
    )(*prefetch, *args)


STATE = [((2 * TILE, HD), F32)] * 3
STATE_SPECS = [IN_VMEM] * 3


def merge_body(*refs):
    sites, outs = refs[:4], refs[4:]
    for h in range(3):
        for t in range(0, SITE, HD):
            n = min(HD, SITE - t)
            levels = [unpack_level(s[h, SITE:], t, n) for s in sites]
            peak = functools.reduce(jnp.maximum, levels)
            weights = [jnp.exp2(level - peak) for level in levels]
            mixed = sum(w * s[h, t : t + n].astype(F32) for w, s in zip(weights, sites))
            mixed = (mixed / sum(weights)).astype(BF16)
            if t < VIDEO:
                for i in range(0, n, 64):
                    outs[(t + i) // 64][h, :64] = mixed[i : i + 64]
            else:
                for out in outs:
                    out[h, 64:] = mixed


def merge(sites):
    return pl.pallas_call(
        merge_body,
        out_shape=[jax.ShapeDtypeStruct((3, 64 + TEXT, HD), BF16)] * 4,
        grid=(1,),
        in_specs=[IN_VMEM] * 4,
        out_specs=[IN_VMEM] * 4,
        compiler_params=pltpu.CompilerParams(vmem_limit_bytes=VMEM // 2),
        name="merge",
    )(*sites)


def finish_body(*refs):
    messages, (video, text) = refs[:4], refs[4:]
    y, zb = lax.axis_index("y"), lax.axis_index("zb")
    for m in range(4):
        group = group_of(m)
        video[pl.ds(group * 3, 3)] = messages[m][:, :64]

        @pl.when(group // 2 == zb)
        def _():
            for h in range(3):
                rows = messages[m][h, 64:].astype(F32)
                own = jnp.zeros((4, HD), F32)
                for i in range(4):
                    own = jnp.where(y == i, rows[4 * i : 4 * i + 4], own)
                text[lax.rem(group, 2) * 3 + h] = own.astype(BF16)


def finish(messages):
    return pl.pallas_call(
        finish_body,
        out_shape=[jax.ShapeDtypeStruct((12, 64, HD), BF16), jax.ShapeDtypeStruct((6, 4, HD), BF16)],
        grid=(1,),
        in_specs=[IN_VMEM] * 4,
        out_specs=[whole(12, 64, HD), whole(6, 4, HD)],
        compiler_params=pltpu.CompilerParams(vmem_limit_bytes=VMEM // 2),
        name="finish",
    )(*messages)


def local(video_q, video_k, video_v, positions, text_q, text_k, text_v, text_count):
    flat = lambda a: jnp.transpose(a, (1, 0, 2))
    out = prepare(flat(video_q), flat(video_k), flat(video_v), positions, flat(text_q), flat(text_k), flat(text_v))
    own, text, text_rows = out[:4], out[4], out[5]
    m = [own[0]] + [shift(own[i], "y", MOVES[i]) for i in range(1, 4)]
    block = jnp.concatenate([text] + [v[:2] for v in m], axis=2)
    right, left = z_shift(block, 1), z_shift(block, -1)
    site = jnp.concatenate([v[2] for v in m] + [text_rows], axis=1)
    queries = jnp.concatenate([site] + [shift(site, "x", -d) for d in MOVES[1:]], axis=1)

    right2, left2 = z_shift(right, 1), z_shift(left, -1)
    state = attend(
        first_body,
        "attend_first",
        [block, right],
        [queries],
        [TILE_SPEC],
        STATE,
        STATE_SPECS,
    )
    right2, left2, *state = lax.optimization_barrier((right2, left2, *state))
    right3, left3 = z_shift(right2, 1), z_shift(left2, -1)
    specs = [TILE_SPEC] + STATE_SPECS
    state = attend(next_body, "attend_2", [left, right2, left2], [queries, *state], specs, STATE, STATE_SPECS)
    right3, left3, *state = lax.optimization_barrier((right3, left3, *state))
    far_k, far_v = z_shift(right3[0], 1), z_shift(left3[1], -1)
    state = attend(next_body, "attend_3", [right3, left3], [queries, *state], specs, STATE, STATE_SPECS)
    sites = attend(
        last_body,
        "attend_last",
        [far_k, far_v],
        [queries, *state],
        specs,
        [((SITE + STATS, HD), BF16)] * 4,
        [head_spec(SITE + STATS, HD)] * 4,
        prefetch=(text_count,),
        texts=[block, right, left, right2, left2, right3, left3, far_k, far_v],
    )
    done = merge([sites[0]] + [shift(sites[i], "x", MOVES[i]) for i in range(1, 4)])
    video, text = finish([done[0]] + [shift(done[m], "y", -MOVES[m]) for m in range(1, 4)])
    return flat(video), flat(text)


def solution(mesh):
    fine = Mesh(mesh.devices.reshape(2, 4, 2, 2, 4, 2), ("grp", "x", "za", "zp", "y", "zb"))
    ctx = ("x", "za", "zp", "y")
    tokens = P(ctx + ("zb",), "grp", None)
    text = P(None, ("grp", "zb"), None)
    return jax.shard_map(
        local,
        mesh=fine,
        in_specs=(tokens, tokens, tokens, P(None, ctx + ("zb",)), text, text, text, P()),
        out_specs=(tokens, P(ctx, ("grp", "zb"), None)),
        check_vma=False,
    )
```
